32 devices in a mesh: case: 2 (over y), ax: 16 (over z, x, core).
Axes of the slice: x: 2, y: 2, z: 4, core: 2. Of those that a mesh axis runs over, the one named last changes fastest.
Arguments:
- checkpoint: float32 [32, 384, 1536], P(('case', 'ax')), parts along dimension 0, may hold values from -6 to 6
- cotangent: float32 [32, 384, 1536], P(('case', 'ax')), parts along dimension 0, may hold values from -6 to 6
- amplitudes: float32 [512], P('case'), parts along dimension 0, may hold values from -6 to 6
- patch_ids: int32 [32, 1536], P(('case', 'ax')), parts along dimension 0, may hold values from 0 to 255
- substep: int32 [2], P('case'), parts along dimension 0, may hold values from 0 to 2
- axial_speed: float32 [384], replicated, may hold values from 0.5 to 1.5
- radial_diffusion: float32 [384], replicated, may hold values from 0.05 to 0.3
- azimuth_diffusion: float32 [384], replicated, may hold values from 0.05 to 0.3
Outputs:
- advanced: float32 [32, 384, 1536], P(('case', 'ax')), parts along dimension 0
- adjoint_state: float32 [32, 384, 1536], P(('case', 'ax')), parts along dimension 0
- actuation_grad: float32 [512], P('case'), parts along dimension 0
The draws below stay inside these ranges and needn't reach their ends.
There are 2 independent parts, one for each index of `case`. The reference program is written for one: setup_inputs(seed, part) draws one part's arguments, and reference() takes and returns one part's arrays. A program takes and returns all parts, laid end to end along the dimension named above; an argument that names none is the same for every part. Nothing has to cross between parts.
All inputs are finite; a program needn't handle non-finite values.
Results may differ from the reference program's by a relative error of at most 0.00002.
Values sent between devices are 32-bit elements; how exact they have to be, the bound alone decides.
No kernel may reach another device: no remote copies, remote signals or barrier semaphores. Data moves between devices by JAX's collectives and lax.ppermute only.
A program may use at most 64 MiB of HBM per device.

```python
import math
import jax
import jax.numpy as jnp

NR = 384
NT = 1536
P_SIZE = 256
NZ = 16


def touch_ends(values, own_key, low, high):
    longest = values.shape.index(max(values.shape))
    spots = []
    for shift in (0, 1):
        where = [jax.random.randint(jax.random.fold_in(own_key, axis), (), 0, length) for axis, length in enumerate(values.shape)]
        where[longest] = (where[longest] + shift) % values.shape[longest]
        spots.append(tuple(where))
    return values.at[spots[0]].set(low).at[spots[1]].set(high)


def steps_of(key, extent, split, least, high):
    gain = 1.0
    for axis_at, parts in split:
        steps = jax.random.uniform(jax.random.fold_in(jax.random.fold_in(key, 6), axis_at), (parts,), jnp.float32, least / len(split), high / len(split))
        gain = gain * jnp.repeat(jnp.exp(steps), extent[axis_at] // parts).reshape((-1,) + (1,) * (len(extent) - 1 - axis_at))
    return gain


def gaussian(own_key, extent, deviation, most, shards=(), held_as=jnp.bfloat16):
    loudness = steps_of(own_key, extent, shards, -0.22, 0.18) if shards else 1.0
    values = jax.random.normal(own_key, extent, jnp.float32) * deviation * loudness
    return jnp.minimum(jnp.maximum(values, -most), most).astype(held_as)


def setup_inputs(seed: int = 0, part: int = 0) -> dict:
    key_list = jax.random.split(jax.random.key(seed), 9)
    own_keys = jax.random.split(jax.random.fold_in(key_list[8], part), 9)
    return {
        "checkpoint": gaussian(own_keys[0], (NZ, NR, NT), 1.0, 6.0, ((0, 16),), jnp.float32),
        "cotangent": gaussian(own_keys[1], (NZ, NR, NT), 1.0, 6.0, ((0, 16),), jnp.float32),
        "amplitudes": gaussian(own_keys[2], (P_SIZE,), 1.0, 6.0, (), jnp.float32),
        "patch_ids": touch_ends(jax.random.randint(own_keys[3], (NZ, NT), 0, P_SIZE), jax.random.fold_in(own_keys[3], 1), 0, P_SIZE - 1).astype(jnp.int32),
        "substep": jax.random.randint(own_keys[4], (1,), 0, 3).astype(jnp.int32),
        "axial_speed": jnp.clip(jax.random.uniform(key_list[5], (NR,), jnp.float32, 0.5, 1.5), 0.5, 1.5),
        "radial_diffusion": jnp.clip(jnp.exp(jax.random.uniform(key_list[6], (NR,), jnp.float32, math.log(0.05), math.log(0.3))), 0.05, 0.3),
        "azimuth_diffusion": jnp.clip(jnp.exp(jax.random.uniform(key_list[7], (NR,), jnp.float32, math.log(0.05), math.log(0.3))), 0.05, 0.3),
    }


time_step = 0.6
dissipation = 2.0

def section_size(substep):
    section_table = jnp.array([1.0 / 3.0, 15.0 / 16.0, 8.0 / 15.0], jnp.float32) * time_step
    selector = (jnp.arange(3, dtype=jnp.int32) == substep[0]).astype(jnp.float32)
    return jnp.sum(section_table * selector)

def advance(checkpoint, amplitudes, patch_ids, axial_speed, radial_diffusion, azimuth_diffusion, step_size):
    speed_rows = axial_speed[None, :, None]
    cell_flux = speed_rows * checkpoint + 0.5 * checkpoint * checkpoint
    next_state = jnp.roll(checkpoint, -1, 0)
    next_flux = jnp.roll(cell_flux, -1, 0)
    face_flux = 0.5 * (cell_flux + next_flux) - 0.5 * dissipation * (next_state - checkpoint)
    axial_term = jnp.roll(face_flux, 1, 0) - face_flux
    wall_value = amplitudes[patch_ids]
    centre_row = jnp.roll(checkpoint[:, :1, :], NT // 2, 2)
    stacked = jnp.concatenate([centre_row, checkpoint, wall_value[:, None, :]], axis=1)
    radial = radial_diffusion[None, :, None] * (stacked[:, 2:, :] - 2.0 * checkpoint + stacked[:, :-2, :])
    azimuthal = azimuth_diffusion[None, :, None] * (jnp.roll(checkpoint, 1, 2) - 2.0 * checkpoint + jnp.roll(checkpoint, -1, 2))
    return checkpoint + step_size * (axial_term + radial + azimuthal)

def reference(checkpoint, cotangent, amplitudes, patch_ids, substep, axial_speed, radial_diffusion, azimuth_diffusion):
    step_size = section_size(substep)

    def forward(flow_now, values):
        return advance(flow_now, values, patch_ids, axial_speed, radial_diffusion, azimuth_diffusion, step_size)
    advanced, pullback = jax.vjp(forward, checkpoint, amplitudes)
    adjoint_state, gradient = pullback(cotangent)
    norm_factor = (P_SIZE / (NZ * NT)) ** 0.5
    return (advanced, adjoint_state, gradient * norm_factor)
```

```python
import functools

import jax
import jax.numpy as jnp
from jax import lax
from jax.experimental import pallas as pl
from jax.experimental.pallas import tpu as pltpu
from jax.sharding import PartitionSpec as P

time_step = 0.6
dissipation = 2.0

STATE_CHUNKS = 1
COT_CHUNKS = 4
BLOCK_ROWS = 48


def section_size(substep):
    section_table = jnp.array([1.0 / 3.0, 15.0 / 16.0, 8.0 / 15.0], jnp.float32) * time_step
    selector = (jnp.arange(3, dtype=jnp.int32) == substep[0]).astype(jnp.float32)
    return jnp.sum(section_table * selector)


def on_pairs(count):
    return [(i, i ^ 1) for i in range(count)]


def off_pairs(count):
    return [(i, (i + 1) % count if i % 2 else (i - 1) % count) for i in range(count)]


def all_sum(value, axis):
    count = lax.axis_size(axis)
    if count & (count - 1):
        return lax.psum(value, axis)
    step = 1
    while step < count:
        value = value + lax.ppermute(value, axis, [(i, i ^ step) for i in range(count)])
        step *= 2
    return value


def state_update(scal, base, near, far, speed, out):
    step, side = scal[0], scal[1]
    u = speed[...]
    a, b = near[0], far[0]
    flux = b * (u + 0.5 * b) - a * (u + 0.5 * a)
    out[0] = base[0] + step * (a + b + (0.5 * side) * flux)


def cot_update(scal, base, near, far, state, speed, out):
    step, side = scal[0], scal[1]
    a, b = near[0], far[0]
    slope = (0.5 * side) * (speed[...] + state[0])
    out[0] = base[0] + step * (a + b + slope * (a - b))


def chunk_update(body, scal, base, whole, part, speed, start, rows):
    width = base.shape[2]
    block = min(BLOCK_ROWS, rows)
    first = start // block
    full = pl.BlockSpec((1, block, width), lambda i: (0, first + i, 0))
    piece = pl.BlockSpec((1, block, width), lambda i: (0, i, 0))
    column = pl.BlockSpec((block, 1), lambda i: (first + i, 0))
    return pl.pallas_call(
        body,
        grid=(rows // block,),
        out_shape=jax.ShapeDtypeStruct(base.shape, base.dtype),
        in_specs=[pl.BlockSpec(memory_space=pltpu.SMEM), full]
        + [piece] * len(part)
        + [full] * len(whole)
        + [column],
        out_specs=full,
        input_output_aliases={1: 0},
        cost_estimate=pl.CostEstimate(
            flops=10 * rows * width, bytes_accessed=4 * rows * width * 5, transcendentals=0
        ),
    )(scal, base, *part, *whole, speed)


def local_parts(
    checkpoint, cotangent, amplitudes, patch_ids, radial_diffusion, azimuth_diffusion, step_size
):
    half_turn = checkpoint.shape[2] // 2
    rd = radial_diffusion[None, :, None]
    ad = azimuth_diffusion[None, :, None]
    wall_value = jnp.take(amplitudes, patch_ids, axis=0)
    centre_row = jnp.roll(checkpoint[:, :1, :], half_turn, 2)
    stacked = jnp.concatenate([centre_row, checkpoint, wall_value[:, None, :]], axis=1)
    radial = rd * (stacked[:, 2:, :] - 2.0 * checkpoint + stacked[:, :-2, :])
    azimuthal = ad * (jnp.roll(checkpoint, 1, 2) - 2.0 * checkpoint + jnp.roll(checkpoint, -1, 2))
    state_base = checkpoint + step_size * (radial + azimuthal - dissipation * checkpoint)

    weighted = rd * cotangent
    across = jnp.roll(weighted[:, :1, :], half_turn, 2)
    above = jnp.concatenate([weighted[:, 1:, :], jnp.zeros_like(weighted[:, :1, :])], axis=1)
    below = jnp.concatenate([across, weighted[:, :-1, :]], axis=1)
    radial_adj = above - 2.0 * weighted + below
    azimuthal_adj = ad * (
        jnp.roll(cotangent, 1, 2) - 2.0 * cotangent + jnp.roll(cotangent, -1, 2)
    )
    cot_base = cotangent + step_size * (radial_adj + azimuthal_adj - dissipation * cotangent)
    return state_base, cot_base


def local(
    checkpoint,
    cotangent,
    amplitudes,
    patch_ids,
    substep,
    axial_speed,
    radial_diffusion,
    azimuth_diffusion,
):
    count = lax.axis_size("ax")
    rows = checkpoint.shape[1]
    near, far = on_pairs(count), off_pairs(count)

    def exchange(value, pieces):
        size = rows // pieces
        return [
            (
                lax.ppermute(value[:, n * size : (n + 1) * size], "ax", far),
                lax.ppermute(value[:, n * size : (n + 1) * size], "ax", near),
            )
            for n in range(pieces)
        ]

    state_halo = exchange(checkpoint, STATE_CHUNKS)
    cot_halo = exchange(cotangent, COT_CHUNKS)

    step_size = section_size(substep)
    patches = amplitudes.shape[0]
    side = 1.0 - 2.0 * (lax.axis_index("ax") % 2).astype(jnp.float32)
    scal = jnp.stack([step_size, side])
    speed = axial_speed[:, None]

    edge_rows = cotangent[:, -1, :].reshape(-1)
    binned = jax.ops.segment_sum(edge_rows, patch_ids.reshape(-1), num_segments=patches)
    total_cells = checkpoint.shape[0] * count * checkpoint.shape[2]
    norm_factor = (patches / total_cells) ** 0.5
    gradient = all_sum(step_size * radial_diffusion[-1] * binned, "ax") * norm_factor

    advanced, adjoint = local_parts(
        checkpoint, cotangent, amplitudes, patch_ids, radial_diffusion, azimuth_diffusion, step_size
    )
    size = rows // STATE_CHUNKS
    for n, (b, a) in enumerate(state_halo):
        advanced = chunk_update(state_update, scal, advanced, [], [a, b], speed, n * size, size)
    size = rows // COT_CHUNKS
    for n, (b, a) in enumerate(cot_halo):
        adjoint = chunk_update(
            cot_update, scal, adjoint, [checkpoint], [a, b], speed, n * size, size
        )
    return (advanced, adjoint, gradient)


def solution(mesh):
    placed = (
        P(("case", "ax"), None, None),
        P(("case", "ax"), None, None),
        P("case"),
        P(("case", "ax"), None),
        P("case"),
        P(),
        P(),
        P(),
    )
    return jax.shard_map(
        local,
        mesh=mesh,
        in_specs=placed,
        out_specs=(P(("case", "ax"), None, None), P(("case", "ax"), None, None), P("case")),
        check_vma=False,
    )
```

```python
import math

import jax
import jax.numpy as jnp
from jax import lax
from jax.experimental import pallas as pl
from jax.experimental.pallas import tpu as pltpu
from jax.sharding import PartitionSpec as P

time_step = 0.6
dissipation = 2.0

STATE_PARTS = 4
STATE_CUTS = (0, 3, 4)
BLOCK_ROWS = 48


def section_size(substep):
    section_table = jnp.array([1.0 / 3.0, 15.0 / 16.0, 8.0 / 15.0], jnp.float32) * time_step
    selector = (jnp.arange(3, dtype=jnp.int32) == substep[0]).astype(jnp.float32)
    return jnp.sum(section_table * selector)


def on_pairs(count):
    return [(i, i ^ 1) for i in range(count)]


def off_pairs(count):
    return [(i, (i + 1) % count if i % 2 else (i - 1) % count) for i in range(count)]


def state_near(scal, base, near, speed, out):
    step, side = scal[0], scal[1]
    x = near[0]
    out[0] = base[0] + step * (x - (0.5 * side) * (x * (speed[...] + 0.5 * x)))


def state_far(scal, base, far, speed, out):
    step, side = scal[0], scal[1]
    x = far[0]
    out[0] = base[0] + step * (x + (0.5 * side) * (x * (speed[...] + 0.5 * x)))


def cot_near(scal, base, near, state, speed, out):
    step, side = scal[0], scal[1]
    out[0] = base[0] + step * near[0] * (1.0 + (0.5 * side) * (speed[...] + state[0]))


def cot_far(scal, base, far, state, speed, out):
    step, side = scal[0], scal[1]
    out[0] = base[0] + step * far[0] * (1.0 - (0.5 * side) * (speed[...] + state[0]))


def add_rows(body, scal, base, part, whole, speed, start):
    rows, width = part.shape[1:]
    block = math.gcd(BLOCK_ROWS, rows)
    first = start // block
    full = pl.BlockSpec((1, block, width), lambda i: (0, first + i, 0))
    piece = pl.BlockSpec((1, block, width), lambda i: (0, i, 0))
    column = pl.BlockSpec((block, 1), lambda i: (first + i, 0))
    return pl.pallas_call(
        body,
        grid=(rows // block,),
        out_shape=jax.ShapeDtypeStruct(base.shape, base.dtype),
        in_specs=[pl.BlockSpec(memory_space=pltpu.SMEM), full, piece]
        + [full] * len(whole)
        + [column],
        out_specs=full,
        input_output_aliases={1: 0},
        cost_estimate=pl.CostEstimate(
            flops=10 * rows * width, bytes_accessed=4 * rows * width * 4, transcendentals=0
        ),
    )(scal, base, part, *whole, speed)


def local_parts(
    checkpoint, cotangent, amplitudes, patch_ids, radial_diffusion, azimuth_diffusion, step_size
):
    half_turn = checkpoint.shape[2] // 2
    rd = radial_diffusion[None, :, None]
    ad = azimuth_diffusion[None, :, None]
    wall_value = jnp.take(amplitudes, patch_ids, axis=0)
    centre_row = jnp.roll(checkpoint[:, :1, :], half_turn, 2)
    stacked = jnp.concatenate([centre_row, checkpoint, wall_value[:, None, :]], axis=1)
    radial = rd * (stacked[:, 2:, :] - 2.0 * checkpoint + stacked[:, :-2, :])
    azimuthal = ad * (jnp.roll(checkpoint, 1, 2) - 2.0 * checkpoint + jnp.roll(checkpoint, -1, 2))
    state_base = checkpoint + step_size * (radial + azimuthal - dissipation * checkpoint)

    weighted = rd * cotangent
    across = jnp.roll(weighted[:, :1, :], half_turn, 2)
    above = jnp.concatenate([weighted[:, 1:, :], jnp.zeros_like(weighted[:, :1, :])], axis=1)
    below = jnp.concatenate([across, weighted[:, :-1, :]], axis=1)
    radial_adj = above - 2.0 * weighted + below
    azimuthal_adj = ad * (
        jnp.roll(cotangent, 1, 2) - 2.0 * cotangent + jnp.roll(cotangent, -1, 2)
    )
    cot_base = cotangent + step_size * (radial_adj + azimuthal_adj - dissipation * cotangent)
    return state_base, cot_base


def local(
    checkpoint,
    cotangent,
    amplitudes,
    patch_ids,
    substep,
    axial_speed,
    radial_diffusion,
    azimuth_diffusion,
):
    count = lax.axis_size("ax")
    rows = checkpoint.shape[1]
    near, far = on_pairs(count), off_pairs(count)

    cot_far_rows = lax.ppermute(cotangent, "ax", far)
    cot_near_rows = lax.ppermute(cotangent, "ax", near)
    state_near_rows = lax.ppermute(checkpoint, "ax", near)

    step_size = section_size(substep)
    patches = amplitudes.shape[0]
    side = 1.0 - 2.0 * (lax.axis_index("ax") % 2).astype(jnp.float32)
    scal = jnp.stack([step_size, side])
    speed = axial_speed[:, None]

    late, cot_near_rows = lax.optimization_barrier((checkpoint, cot_near_rows))
    edges = [rows * n // STATE_PARTS for n in STATE_CUTS]
    state_far_rows = [
        lax.ppermute(late[:, low:high], "ax", far) for low, high in zip(edges, edges[1:])
    ]

    edge_rows = cotangent[:, -1, :].reshape(-1)
    binned = jax.ops.segment_sum(edge_rows, patch_ids.reshape(-1), num_segments=patches)
    total_cells = checkpoint.shape[0] * count * checkpoint.shape[2]
    norm_factor = (patches / total_cells) ** 0.5
    gradient = lax.all_gather(step_size * radial_diffusion[-1] * binned, "ax")
    gradient = jnp.sum(gradient, axis=0) * norm_factor

    advanced, adjoint = local_parts(
        checkpoint, cotangent, amplitudes, patch_ids, radial_diffusion, azimuth_diffusion, step_size
    )
    adjoint = add_rows(cot_near, scal, adjoint, cot_near_rows, [checkpoint], speed, 0)
    advanced = add_rows(state_near, scal, advanced, state_near_rows, [], speed, 0)
    adjoint = add_rows(cot_far, scal, adjoint, cot_far_rows, [checkpoint], speed, 0)
    for low, part in zip(edges, state_far_rows):
        advanced = add_rows(state_far, scal, advanced, part, [], speed, low)
    return (advanced, adjoint, gradient)


def solution(mesh):
    placed = (
        P(("case", "ax"), None, None),
        P(("case", "ax"), None, None),
        P("case"),
        P(("case", "ax"), None),
        P("case"),
        P(),
        P(),
        P(),
    )
    return jax.shard_map(
        local,
        mesh=mesh,
        in_specs=placed,
        out_specs=(P(("case", "ax"), None, None), P(("case", "ax"), None, None), P("case")),
        check_vma=False,
    )
```

```python
import math

import jax
import jax.numpy as jnp
from jax import lax
from jax.experimental import pallas as pl
from jax.experimental.pallas import tpu as pltpu
from jax.sharding import PartitionSpec as P

time_step = 0.6
dissipation = 2.0

STATE_PARTS = 4
STATE_CUTS = (0, 3, 4)
LOCAL_ROWS = 64
ADD_ROWS = 96
SUB = 8


def section_size(substep):
    section_table = jnp.array([1.0 / 3.0, 15.0 / 16.0, 8.0 / 15.0], jnp.float32) * time_step
    selector = (jnp.arange(3, dtype=jnp.int32) == substep[0]).astype(jnp.float32)
    return jnp.sum(section_table * selector)


def on_pairs(count):
    return [(i, i ^ 1) for i in range(count)]


def off_pairs(count):
    return [(i, (i + 1) % count if i % 2 else (i - 1) % count) for i in range(count)]


def wall_kernel(ids, amplitudes, edge, wall, bins):
    patches, cells = amplitudes.shape[1], ids.shape[1]
    patch = lax.broadcasted_iota(jnp.int32, (patches, cells), 0)
    hit = jnp.where(patch == ids[...], 1.0, 0.0).astype(jnp.float32)
    values = jnp.broadcast_to(amplitudes[...], (SUB, patches))
    wall[...] = lax.dot_general(
        values,
        hit,
        (((1,), (0,)), ((), ())),
        precision=lax.Precision.HIGHEST,
        preferred_element_type=jnp.float32,
    )[:1]
    bins[...] = lax.dot_general(
        edge[0],
        hit,
        (((1,), (1,)), ((), ())),
        precision=lax.Precision.HIGHEST,
        preferred_element_type=jnp.float32,
    )[SUB - 1 :]


def wall_and_bins(patch_ids, amplitudes, cotangent):
    rows, cells = cotangent.shape[1:]
    patches = amplitudes.shape[0]
    return pl.pallas_call(
        wall_kernel,
        grid=(1,),
        out_shape=(
            jax.ShapeDtypeStruct((1, cells), jnp.float32),
            jax.ShapeDtypeStruct((1, patches), jnp.float32),
        ),
        in_specs=[
            pl.BlockSpec((1, cells), lambda i: (0, 0)),
            pl.BlockSpec((1, patches), lambda i: (0, 0)),
            pl.BlockSpec((1, SUB, cells), lambda i: (0, rows // SUB - 1, 0)),
        ],
        out_specs=(
            pl.BlockSpec((1, cells), lambda i: (0, 0)),
            pl.BlockSpec((1, patches), lambda i: (0, 0)),
        ),
        compiler_params=pltpu.CompilerParams(vmem_limit_bytes=40 << 20),
    )(patch_ids, amplitudes[None], cotangent)


def local_kernel(scal, q, q_up, q_down, q_near, c, c_up, c_down, c_near, wall, coef, q_out, c_out):
    block, width = q.shape[1:]
    step, side = scal[0], scal[1]
    here, last = pl.program_id(0), pl.num_programs(0) - 1
    u, rd, ad = coef[:, 0:1], coef[:, 1:2], coef[:, 2:3]
    row = lax.broadcasted_iota(jnp.int32, (block, 1), 0)

    def around(x, up, down):
        above = jnp.where(row == 0, up, pltpu.roll(x, 1, 0))
        below = jnp.where(row == block - 1, down, pltpu.roll(x, block - 1, 0))
        return above, below

    def sides(x):
        return pltpu.roll(x, 1, 1) + pltpu.roll(x, width - 1, 1)

    x = q[0]
    first_row = pltpu.roll(x[:1], width // 2, 1)
    up = jnp.where(here == 0, first_row, q_up[0, SUB - 1 :])
    down = jnp.where(here == last, wall[...], q_down[0, :1])
    above, below = around(x, up, down)
    near = q_near[0]
    axial = near - (0.5 * side) * (near * (u + 0.5 * near)) - dissipation * x
    q_out[0] = x + step * (
        axial + rd * (above + below - 2.0 * x) + ad * (sides(x) - 2.0 * x)
    )

    y = c[0]
    weighted = rd * y
    before, after = coef_rows(coef)
    first_row = pltpu.roll(weighted[:1], width // 2, 1)
    up = jnp.where(here == 0, first_row, before * c_up[0, SUB - 1 :])
    down = jnp.where(here == last, 0.0, after * c_down[0, :1])
    above, below = around(weighted, up, down)
    axial = c_near[0] * (1.0 + (0.5 * side) * (u + x)) - dissipation * y
    c_out[0] = y + step * (
        axial + (above + below - 2.0 * weighted) + ad * (sides(y) - 2.0 * y)
    )


def coef_rows(coef):
    return coef[0:1, 3:4], coef[0:1, 4:5]


def local_parts(scal, q, q_near, c, c_near, wall, coef):
    rows, width = q.shape[1:]
    block = math.gcd(LOCAL_ROWS, rows)
    tiles, total = block // SUB, rows // SUB
    full = pl.BlockSpec((1, block, width), lambda i: (0, i, 0))
    up = pl.BlockSpec((1, SUB, width), lambda i: (0, jnp.maximum(i * tiles - 1, 0), 0))
    down = pl.BlockSpec((1, SUB, width), lambda i: (0, jnp.minimum((i + 1) * tiles, total - 1), 0))
    rd = coef[:, 1]
    before, after = jnp.roll(rd, 1), jnp.roll(rd, -block)
    coef = jnp.concatenate([coef, before[:, None], after[:, None]], axis=1)
    shape = jax.ShapeDtypeStruct(q.shape, q.dtype)
    return pl.pallas_call(
        local_kernel,
        grid=(rows // block,),
        out_shape=(shape, shape),
        in_specs=[pl.BlockSpec(memory_space=pltpu.SMEM)]
        + [full, up, down, full] * 2
        + [pl.BlockSpec((1, width), lambda i: (0, 0))]
        + [pl.BlockSpec((block, coef.shape[1]), lambda i: (i, 0))],
        out_specs=(full, full),
        compiler_params=pltpu.CompilerParams(vmem_limit_bytes=40 << 20),
        cost_estimate=pl.CostEstimate(
            flops=50 * rows * width, bytes_accessed=4 * rows * width * 6, transcendentals=0
        ),
    )(scal, q, q, q, q_near, c, c, c, c_near, wall, coef)


def state_far(scal, base, far, coef, out):
    step, side = scal[0], scal[1]
    x = far[0]
    out[0] = base[0] + step * (x + (0.5 * side) * (x * (coef[:, 0:1] + 0.5 * x)))


def state_last(scal, base, far, mine, other, coef, out, gradient):
    state_far(scal, base, far, coef, out)
    gradient[...] = scal[2] * (mine[...] + other[...])


def cot_far(scal, base, far, state, coef, out):
    step, side = scal[0], scal[1]
    out[0] = base[0] + step * far[0] * (1.0 - (0.5 * side) * (coef[:, 0:1] + state[0]))


def add_rows(body, scal, base, part, whole, coef, start, small=()):
    rows, width = part.shape[1:]
    block = math.gcd(ADD_ROWS, rows)
    first = start // block
    full = pl.BlockSpec((1, block, width), lambda i: (0, first + i, 0))
    piece = pl.BlockSpec((1, block, width), lambda i: (0, i, 0))
    column = pl.BlockSpec((block, coef.shape[1]), lambda i: (first + i, 0))
    short = [pl.BlockSpec(x.shape, lambda i: (0, 0)) for x in small]
    shape = jax.ShapeDtypeStruct(base.shape, base.dtype)
    return pl.pallas_call(
        body,
        grid=(rows // block,),
        out_shape=(shape, jax.ShapeDtypeStruct(small[0].shape, base.dtype)) if small else shape,
        in_specs=[pl.BlockSpec(memory_space=pltpu.SMEM), full, piece]
        + short
        + [full] * len(whole)
        + [column],
        out_specs=(full, short[0]) if small else full,
        input_output_aliases={1: 0},
        compiler_params=pltpu.CompilerParams(vmem_limit_bytes=40 << 20),
        cost_estimate=pl.CostEstimate(
            flops=10 * rows * width, bytes_accessed=4 * rows * width * 4, transcendentals=0
        ),
    )(scal, base, part, *small, *whole, coef)


def local(
    checkpoint,
    cotangent,
    amplitudes,
    patch_ids,
    substep,
    axial_speed,
    radial_diffusion,
    azimuth_diffusion,
):
    count = lax.axis_size("ax")
    rows = checkpoint.shape[1]
    patches = amplitudes.shape[0]
    near, far = on_pairs(count), off_pairs(count)
    cot_far_rows = lax.ppermute(cotangent, "ax", far)
    cot_near_rows = lax.ppermute(cotangent, "ax", near)
    state_near_rows = lax.ppermute(checkpoint, "ax", near)

    cot_now, cot_near_rows = lax.optimization_barrier((cotangent, cot_near_rows))
    wall, binned = wall_and_bins(patch_ids, amplitudes, cot_now)

    if count & (count - 1) or count < 4:
        binned = lax.psum(binned, "ax")
        other = jnp.zeros_like(binned)
        late = checkpoint
    else:
        for n in [1] + [1 << n for n in range(2, count.bit_length() - 1)]:
            binned = binned + lax.ppermute(binned, "ax", [(i, i ^ n) for i in range(count)])
        late, binned, state_near_rows = lax.optimization_barrier(
            (checkpoint, binned, state_near_rows)
        )
        other = lax.ppermute(binned, "ax", [(i, i ^ 2) for i in range(count)])

    edges = [rows * n // STATE_PARTS for n in STATE_CUTS]
    state_far_rows = [
        lax.ppermute(late[:, low:high], "ax", far) for low, high in zip(edges, edges[1:])
    ]

    step_size = section_size(substep)
    side = 1.0 - 2.0 * (lax.axis_index("ax") % 2).astype(jnp.float32)
    total_cells = checkpoint.shape[0] * count * checkpoint.shape[2]
    norm_factor = (patches / total_cells) ** 0.5
    scal = jnp.stack([step_size, side, step_size * radial_diffusion[-1] * norm_factor])
    coef = jnp.stack([axial_speed, radial_diffusion, azimuth_diffusion], axis=1)

    advanced, adjoint = local_parts(
        scal, checkpoint, state_near_rows, cotangent, cot_near_rows, wall, coef
    )
    adjoint = add_rows(cot_far, scal, adjoint, cot_far_rows, [checkpoint], coef, 0)
    advanced, adjoint = lax.optimization_barrier((advanced, adjoint))
    for low, part in zip(edges[:-2], state_far_rows[:-1]):
        advanced = add_rows(state_far, scal, advanced, part, [], coef, low)
    advanced, gradient = add_rows(
        state_last, scal, advanced, state_far_rows[-1], [], coef, edges[-2], (binned, other)
    )
    return (advanced, adjoint, gradient[0])


def solution(mesh):
    placed = (
        P(("case", "ax"), None, None),
        P(("case", "ax"), None, None),
        P("case"),
        P(("case", "ax"), None),
        P("case"),
        P(),
        P(),
        P(),
    )
    return jax.shard_map(
        local,
        mesh=mesh,
        in_specs=placed,
        out_specs=(P(("case", "ax"), None, None), P(("case", "ax"), None, None), P("case")),
        check_vma=False,
    )
```

```python
import math

import jax
import jax.numpy as jnp
from jax import lax
from jax.experimental import pallas as pl
from jax.experimental.pallas import tpu as pltpu
from jax.sharding import PartitionSpec as P

time_step = 0.6
dissipation = 2.0

STATE_PARTS = 16
STATE_CUTS = (0, 12, 15, 16)
LOCAL_ROWS = 64
ADD_ROWS = 96
SUB = 8


def section_size(substep):
    section_table = jnp.array([1.0 / 3.0, 15.0 / 16.0, 8.0 / 15.0], jnp.float32) * time_step
    selector = (jnp.arange(3, dtype=jnp.int32) == substep[0]).astype(jnp.float32)
    return jnp.sum(section_table * selector)


def on_pairs(count):
    return [(i, i ^ 1) for i in range(count)]


def off_pairs(count):
    return [(i, (i + 1) % count if i % 2 else (i - 1) % count) for i in range(count)]


def wall_kernel(ids, amplitudes, edge, wall, bins):
    patches, cells = amplitudes.shape[1], ids.shape[1]
    patch = lax.broadcasted_iota(jnp.int32, (patches, cells), 0)
    hit = jnp.where(patch == ids[...], 1.0, 0.0).astype(jnp.float32)
    values = jnp.broadcast_to(amplitudes[...], (SUB, patches))
    wall[...] = lax.dot_general(
        values,
        hit,
        (((1,), (0,)), ((), ())),
        precision=lax.Precision.HIGHEST,
        preferred_element_type=jnp.float32,
    )[:1]
    bins[...] = lax.dot_general(
        edge[0],
        hit,
        (((1,), (1,)), ((), ())),
        precision=lax.Precision.HIGHEST,
        preferred_element_type=jnp.float32,
    )[SUB - 1 :]


def wall_and_bins(patch_ids, amplitudes, cotangent):
    rows, cells = cotangent.shape[1:]
    patches = amplitudes.shape[0]
    return pl.pallas_call(
        wall_kernel,
        grid=(1,),
        out_shape=(
            jax.ShapeDtypeStruct((1, cells), jnp.float32),
            jax.ShapeDtypeStruct((1, patches), jnp.float32),
        ),
        in_specs=[
            pl.BlockSpec((1, cells), lambda i: (0, 0)),
            pl.BlockSpec((1, patches), lambda i: (0, 0)),
            pl.BlockSpec((1, SUB, cells), lambda i: (0, rows // SUB - 1, 0)),
        ],
        out_specs=(
            pl.BlockSpec((1, cells), lambda i: (0, 0)),
            pl.BlockSpec((1, patches), lambda i: (0, 0)),
        ),
        compiler_params=pltpu.CompilerParams(vmem_limit_bytes=40 << 20),
    )(patch_ids, amplitudes[None], cotangent)


def local_kernel(scal, q, q_up, q_down, q_near, c, c_up, c_down, c_near, wall, coef, q_out, c_out):
    block, width = q.shape[1:]
    step, side = scal[0], scal[1]
    here, last = pl.program_id(0), pl.num_programs(0) - 1
    u, rd, ad = coef[:, 0:1], coef[:, 1:2], coef[:, 2:3]
    row = lax.broadcasted_iota(jnp.int32, (block, 1), 0)

    def around(x, up, down):
        above = jnp.where(row == 0, up, pltpu.roll(x, 1, 0))
        below = jnp.where(row == block - 1, down, pltpu.roll(x, block - 1, 0))
        return above, below

    def sides(x):
        return pltpu.roll(x, 1, 1) + pltpu.roll(x, width - 1, 1)

    x = q[0]
    first_row = pltpu.roll(x[:1], width // 2, 1)
    up = jnp.where(here == 0, first_row, q_up[0, SUB - 1 :])
    down = jnp.where(here == last, wall[...], q_down[0, :1])
    above, below = around(x, up, down)
    near = q_near[0]
    axial = near - (0.5 * side) * (near * (u + 0.5 * near)) - dissipation * x
    q_out[0] = x + step * (
        axial + rd * (above + below - 2.0 * x) + ad * (sides(x) - 2.0 * x)
    )

    y = c[0]
    weighted = rd * y
    before, after = coef_rows(coef)
    first_row = pltpu.roll(weighted[:1], width // 2, 1)
    up = jnp.where(here == 0, first_row, before * c_up[0, SUB - 1 :])
    down = jnp.where(here == last, 0.0, after * c_down[0, :1])
    above, below = around(weighted, up, down)
    axial = c_near[0] * (1.0 + (0.5 * side) * (u + x)) - dissipation * y
    c_out[0] = y + step * (
        axial + (above + below - 2.0 * weighted) + ad * (sides(y) - 2.0 * y)
    )


def coef_rows(coef):
    return coef[0:1, 3:4], coef[0:1, 4:5]


def local_parts(scal, q, q_near, c, c_near, wall, coef):
    rows, width = q.shape[1:]
    block = math.gcd(LOCAL_ROWS, rows)
    tiles, total = block // SUB, rows // SUB
    full = pl.BlockSpec((1, block, width), lambda i: (0, i, 0))
    up = pl.BlockSpec((1, SUB, width), lambda i: (0, jnp.maximum(i * tiles - 1, 0), 0))
    down = pl.BlockSpec((1, SUB, width), lambda i: (0, jnp.minimum((i + 1) * tiles, total - 1), 0))
    rd = coef[:, 1]
    before, after = jnp.roll(rd, 1), jnp.roll(rd, -block)
    coef = jnp.concatenate([coef, before[:, None], after[:, None]], axis=1)
    shape = jax.ShapeDtypeStruct(q.shape, q.dtype)
    return pl.pallas_call(
        local_kernel,
        grid=(rows // block,),
        out_shape=(shape, shape),
        in_specs=[pl.BlockSpec(memory_space=pltpu.SMEM)]
        + [full, up, down, full] * 2
        + [pl.BlockSpec((1, width), lambda i: (0, 0))]
        + [pl.BlockSpec((block, coef.shape[1]), lambda i: (i, 0))],
        out_specs=(full, full),
        compiler_params=pltpu.CompilerParams(vmem_limit_bytes=40 << 20),
        cost_estimate=pl.CostEstimate(
            flops=50 * rows * width, bytes_accessed=4 * rows * width * 6, transcendentals=0
        ),
    )(scal, q, q, q, q_near, c, c, c, c_near, wall, coef)


def state_far(scal, base, far, coef, out):
    step, side = scal[0], scal[1]
    x = far[0]
    out[0] = base[0] + step * (x + (0.5 * side) * (x * (coef[:, 0:1] + 0.5 * x)))


def state_last(scal, base, far, mine, other, coef, out, gradient):
    state_far(scal, base, far, coef, out)
    gradient[...] = scal[2] * (mine[...] + other[...])


def cot_far(scal, base, far, state, coef, out):
    step, side = scal[0], scal[1]
    out[0] = base[0] + step * far[0] * (1.0 - (0.5 * side) * (coef[:, 0:1] + state[0]))


def add_rows(body, scal, base, part, whole, coef, start, small=()):
    rows, width = part.shape[1:]
    block = rows if rows <= ADD_ROWS else math.gcd(ADD_ROWS, rows)
    first = start // block
    full = pl.BlockSpec((1, block, width), lambda i: (0, first + i, 0))
    piece = pl.BlockSpec((1, block, width), lambda i: (0, i, 0))
    column = pl.BlockSpec((block, coef.shape[1]), lambda i: (first + i, 0))
    short = [pl.BlockSpec(x.shape, lambda i: (0, 0)) for x in small]
    shape = jax.ShapeDtypeStruct(base.shape, base.dtype)
    return pl.pallas_call(
        body,
        grid=(rows // block,),
        out_shape=(shape, jax.ShapeDtypeStruct(small[0].shape, base.dtype)) if small else shape,
        in_specs=[pl.BlockSpec(memory_space=pltpu.SMEM), full, piece]
        + short
        + [full] * len(whole)
        + [column],
        out_specs=(full, short[0]) if small else full,
        input_output_aliases={1: 0},
        compiler_params=pltpu.CompilerParams(vmem_limit_bytes=40 << 20),
        cost_estimate=pl.CostEstimate(
            flops=10 * rows * width, bytes_accessed=4 * rows * width * 4, transcendentals=0
        ),
    )(scal, base, part, *small, *whole, coef)


def local(
    checkpoint,
    cotangent,
    amplitudes,
    patch_ids,
    substep,
    axial_speed,
    radial_diffusion,
    azimuth_diffusion,
):
    count = lax.axis_size("ax")
    rows = checkpoint.shape[1]
    patches = amplitudes.shape[0]
    near, far = on_pairs(count), off_pairs(count)
    cot_far_rows = lax.ppermute(cotangent, "ax", far)
    cot_near_rows = lax.ppermute(cotangent, "ax", near)
    state_near_rows = lax.ppermute(checkpoint, "ax", near)

    cot_now, cot_near_rows = lax.optimization_barrier((cotangent, cot_near_rows))
    wall, binned = wall_and_bins(patch_ids, amplitudes, cot_now)

    if count & (count - 1) or count < 4:
        binned = lax.psum(binned, "ax")
        other = jnp.zeros_like(binned)
        late = checkpoint
    else:
        for n in [1] + [1 << n for n in range(2, count.bit_length() - 1)]:
            binned = binned + lax.ppermute(binned, "ax", [(i, i ^ n) for i in range(count)])
        late, binned, state_near_rows = lax.optimization_barrier(
            (checkpoint, binned, state_near_rows)
        )
        other = lax.ppermute(binned, "ax", [(i, i ^ 3) for i in range(count)])

    edges = [rows * n // STATE_PARTS for n in STATE_CUTS]
    state_far_rows = [
        lax.ppermute(late[:, low:high], "ax", far) for low, high in zip(edges, edges[1:])
    ]

    step_size = section_size(substep)
    side = 1.0 - 2.0 * (lax.axis_index("ax") % 2).astype(jnp.float32)
    total_cells = checkpoint.shape[0] * count * checkpoint.shape[2]
    norm_factor = (patches / total_cells) ** 0.5
    scal = jnp.stack([step_size, side, step_size * radial_diffusion[-1] * norm_factor])
    coef = jnp.stack([axial_speed, radial_diffusion, azimuth_diffusion], axis=1)

    advanced, adjoint = local_parts(
        scal, checkpoint, state_near_rows, cotangent, cot_near_rows, wall, coef
    )
    adjoint = add_rows(cot_far, scal, adjoint, cot_far_rows, [checkpoint], coef, 0)
    advanced, adjoint = lax.optimization_barrier((advanced, adjoint))
    for low, part in zip(edges[:-2], state_far_rows[:-1]):
        advanced = add_rows(state_far, scal, advanced, part, [], coef, low)
    advanced, gradient = add_rows(
        state_last, scal, advanced, state_far_rows[-1], [], coef, edges[-2], (binned, other)
    )
    return (advanced, adjoint, gradient[0])


def solution(mesh):
    placed = (
        P(("case", "ax"), None, None),
        P(("case", "ax"), None, None),
        P("case"),
        P(("case", "ax"), None),
        P("case"),
        P(),
        P(),
        P(),
    )
    return jax.shard_map(
        local,
        mesh=mesh,
        in_specs=placed,
        out_specs=(P(("case", "ax"), None, None), P(("case", "ax"), None, None), P("case")),
        check_vma=False,
    )
```

```python
import math

import jax
import jax.numpy as jnp
from jax import lax
from jax.experimental import pallas as pl
from jax.experimental.pallas import tpu as pltpu
from jax.sharding import PartitionSpec as P

time_step = 0.6
dissipation = 2.0

STATE_PARTS = 16
STATE_CUTS = (0, 12, 15, 16)
LOCAL_ROWS = 64
ADD_ROWS = 96
SUB = 8


def section_size(substep):
    section_table = jnp.array([1.0 / 3.0, 15.0 / 16.0, 8.0 / 15.0], jnp.float32) * time_step
    selector = (jnp.arange(3, dtype=jnp.int32) == substep[0]).astype(jnp.float32)
    return jnp.sum(section_table * selector)


def on_pairs(count):
    return [(i, i ^ 1) for i in range(count)]


def off_pairs(count):
    return [(i, (i + 1) % count if i % 2 else (i - 1) % count) for i in range(count)]


def wall_kernel(ids, amplitudes, edge, wall, bins):
    patches, cells = amplitudes.shape[1], ids.shape[1]
    patch = lax.broadcasted_iota(jnp.int32, (patches, cells), 0)
    hit = jnp.where(patch == ids[...], 1.0, 0.0).astype(jnp.float32)
    values = jnp.broadcast_to(amplitudes[...], (SUB, patches))
    wall[...] = lax.dot_general(
        values,
        hit,
        (((1,), (0,)), ((), ())),
        precision=lax.Precision.HIGHEST,
        preferred_element_type=jnp.float32,
    )[:1]
    bins[...] = lax.dot_general(
        edge[0],
        hit,
        (((1,), (1,)), ((), ())),
        precision=lax.Precision.HIGHEST,
        preferred_element_type=jnp.float32,
    )[SUB - 1 :]


def wall_and_bins(patch_ids, amplitudes, cotangent):
    rows, cells = cotangent.shape[1:]
    patches = amplitudes.shape[0]
    return pl.pallas_call(
        wall_kernel,
        grid=(1,),
        out_shape=(
            jax.ShapeDtypeStruct((1, cells), jnp.float32),
            jax.ShapeDtypeStruct((1, patches), jnp.float32),
        ),
        in_specs=[
            pl.BlockSpec((1, cells), lambda i: (0, 0)),
            pl.BlockSpec((1, patches), lambda i: (0, 0)),
            pl.BlockSpec((1, SUB, cells), lambda i: (0, rows // SUB - 1, 0)),
        ],
        out_specs=(
            pl.BlockSpec((1, cells), lambda i: (0, 0)),
            pl.BlockSpec((1, patches), lambda i: (0, 0)),
        ),
        compiler_params=pltpu.CompilerParams(vmem_limit_bytes=40 << 20),
    )(patch_ids, amplitudes[None], cotangent)


def local_kernel(scal, q, q_up, q_down, q_near, c, c_up, c_down, c_near, wall, coef, q_out, c_out):
    block, width = q.shape[1:]
    step, side = scal[0], scal[1]
    here, last = pl.program_id(0), pl.num_programs(0) - 1
    u, rd, ad = coef[:, 0:1], coef[:, 1:2], coef[:, 2:3]
    row = lax.broadcasted_iota(jnp.int32, (block, 1), 0)

    def around(x, up, down):
        above = jnp.where(row == 0, up, pltpu.roll(x, 1, 0))
        below = jnp.where(row == block - 1, down, pltpu.roll(x, block - 1, 0))
        return above, below

    def sides(x):
        return pltpu.roll(x, 1, 1) + pltpu.roll(x, width - 1, 1)

    x = q[0]
    first_row = pltpu.roll(x[:1], width // 2, 1)
    up = jnp.where(here == 0, first_row, q_up[0, SUB - 1 :])
    down = jnp.where(here == last, wall[...], q_down[0, :1])
    above, below = around(x, up, down)
    near = q_near[0]
    axial = near - (0.5 * side) * (near * (u + 0.5 * near)) - dissipation * x
    q_out[0] = x + step * (
        axial + rd * (above + below - 2.0 * x) + ad * (sides(x) - 2.0 * x)
    )

    y = c[0]
    weighted = rd * y
    before, after = coef_rows(coef)
    first_row = pltpu.roll(weighted[:1], width // 2, 1)
    up = jnp.where(here == 0, first_row, before * c_up[0, SUB - 1 :])
    down = jnp.where(here == last, 0.0, after * c_down[0, :1])
    above, below = around(weighted, up, down)
    axial = c_near[0] * (1.0 + (0.5 * side) * (u + x)) - dissipation * y
    c_out[0] = y + step * (
        axial + (above + below - 2.0 * weighted) + ad * (sides(y) - 2.0 * y)
    )


def coef_rows(coef):
    return coef[0:1, 3:4], coef[0:1, 4:5]


def local_parts(scal, q, q_near, c, c_near, wall, coef):
    rows, width = q.shape[1:]
    block = math.gcd(LOCAL_ROWS, rows)
    tiles, total = block // SUB, rows // SUB
    full = pl.BlockSpec((1, block, width), lambda i: (0, i, 0))
    up = pl.BlockSpec((1, SUB, width), lambda i: (0, jnp.maximum(i * tiles - 1, 0), 0))
    down = pl.BlockSpec((1, SUB, width), lambda i: (0, jnp.minimum((i + 1) * tiles, total - 1), 0))
    rd = coef[:, 1]
    before, after = jnp.roll(rd, 1), jnp.roll(rd, -block)
    coef = jnp.concatenate([coef, before[:, None], after[:, None]], axis=1)
    shape = jax.ShapeDtypeStruct(q.shape, q.dtype)
    return pl.pallas_call(
        local_kernel,
        grid=(rows // block,),
        out_shape=(shape, shape),
        in_specs=[pl.BlockSpec(memory_space=pltpu.SMEM)]
        + [full, up, down, full] * 2
        + [pl.BlockSpec((1, width), lambda i: (0, 0))]
        + [pl.BlockSpec((block, coef.shape[1]), lambda i: (i, 0))],
        out_specs=(full, full),
        compiler_params=pltpu.CompilerParams(vmem_limit_bytes=40 << 20),
        cost_estimate=pl.CostEstimate(
            flops=50 * rows * width, bytes_accessed=4 * rows * width * 6, transcendentals=0
        ),
    )(scal, q, q, q, q_near, c, c, c, c_near, wall, coef)


def state_far(scal, base, far, coef, out):
    step, side = scal[0], scal[1]
    x = far[0]
    out[0] = base[0] + step * (x + (0.5 * side) * (x * (coef[:, 0:1] + 0.5 * x)))


def cot_far(scal, base, far, state, coef, out):
    step, side = scal[0], scal[1]
    out[0] = base[0] + step * far[0] * (1.0 - (0.5 * side) * (coef[:, 0:1] + state[0]))


def add_rows(body, scal, base, part, whole, coef, start):
    rows, width = part.shape[1:]
    block = rows if rows <= ADD_ROWS else math.gcd(ADD_ROWS, rows)
    first = start // block
    full = pl.BlockSpec((1, block, width), lambda i: (0, first + i, 0))
    piece = pl.BlockSpec((1, block, width), lambda i: (0, i, 0))
    column = pl.BlockSpec((block, coef.shape[1]), lambda i: (first + i, 0))
    return pl.pallas_call(
        body,
        grid=(rows // block,),
        out_shape=jax.ShapeDtypeStruct(base.shape, base.dtype),
        in_specs=[pl.BlockSpec(memory_space=pltpu.SMEM), full, piece]
        + [full] * len(whole)
        + [column],
        out_specs=full,
        input_output_aliases={1: 0},
        compiler_params=pltpu.CompilerParams(vmem_limit_bytes=40 << 20),
        cost_estimate=pl.CostEstimate(
            flops=10 * rows * width, bytes_accessed=4 * rows * width * 4, transcendentals=0
        ),
    )(scal, base, part, *whole, coef)


def local(
    checkpoint,
    cotangent,
    amplitudes,
    patch_ids,
    substep,
    axial_speed,
    radial_diffusion,
    azimuth_diffusion,
):
    count = lax.axis_size("ax")
    rows = checkpoint.shape[1]
    patches = amplitudes.shape[0]
    near, far = on_pairs(count), off_pairs(count)
    cot_far_rows = lax.ppermute(cotangent, "ax", far)
    cot_near_rows = lax.ppermute(cotangent, "ax", near)
    state_near_rows = lax.ppermute(checkpoint, "ax", near)

    wall, binned = wall_and_bins(patch_ids, amplitudes, cotangent)

    late, state_near_rows = lax.optimization_barrier((checkpoint, state_near_rows))
    if count & (count - 1) or count < 4:
        binned = lax.psum(binned, "ax")
    else:
        for n in [1] + [1 << n for n in range(2, count.bit_length() - 1)]:
            binned = binned + lax.ppermute(binned, "ax", [(i, i ^ n) for i in range(count)])
        lead = [i for i in range(count) if i % 4 in (0, 3)]
        other = lax.ppermute(binned, "ax", [(i, i ^ 3) for i in lead])
        whole = binned + other
        given = lax.ppermute(whole, "ax", [(i, i ^ 1) for i in lead])
        place = lax.axis_index("ax") % 4
        binned = jnp.where((place == 0) | (place == 3), whole, given)

    edges = [rows * n // STATE_PARTS for n in STATE_CUTS]
    state_far_rows = [
        lax.ppermute(late[:, low:high], "ax", far) for low, high in zip(edges, edges[1:])
    ]

    step_size = section_size(substep)
    side = 1.0 - 2.0 * (lax.axis_index("ax") % 2).astype(jnp.float32)
    total_cells = checkpoint.shape[0] * count * checkpoint.shape[2]
    norm_factor = (patches / total_cells) ** 0.5
    gradient = (step_size * radial_diffusion[-1] * norm_factor) * binned[0]
    scal = jnp.stack([step_size, side])
    coef = jnp.stack([axial_speed, radial_diffusion, azimuth_diffusion], axis=1)

    advanced, adjoint = local_parts(
        scal, checkpoint, state_near_rows, cotangent, cot_near_rows, wall, coef
    )
    adjoint = add_rows(cot_far, scal, adjoint, cot_far_rows, [checkpoint], coef, 0)
    advanced, adjoint = lax.optimization_barrier((advanced, adjoint))
    for low, part in zip(edges[:-2], state_far_rows[:-1]):
        advanced = add_rows(state_far, scal, advanced, part, [], coef, low)
    advanced, gradient = lax.optimization_barrier((advanced, gradient))
    low, x = edges[-2], state_far_rows[-1]
    last = advanced[:, low:] + step_size * (
        x + (0.5 * side) * (x * (axial_speed[None, low:, None] + 0.5 * x))
    )
    advanced = lax.dynamic_update_slice(advanced, last, (0, low, 0))
    return (advanced, adjoint, gradient)


def solution(mesh):
    placed = (
        P(("case", "ax"), None, None),
        P(("case", "ax"), None, None),
        P("case"),
        P(("case", "ax"), None),
        P("case"),
        P(),
        P(),
        P(),
    )
    return jax.shard_map(
        local,
        mesh=mesh,
        in_specs=placed,
        out_specs=(P(("case", "ax"), None, None), P(("case", "ax"), None, None), P("case")),
        check_vma=False,
    )
```

```python
import math

import jax
import jax.numpy as jnp
from jax import lax
from jax.experimental import pallas as pl
from jax.experimental.pallas import tpu as pltpu
from jax.sharding import PartitionSpec as P

time_step = 0.6
dissipation = 2.0

STATE_PARTS = 16
STATE_CUTS = (0, 12, 15, 16)
LOCAL_ROWS = 64
ADD_ROWS = 96
SUB = 8


def section_size(substep):
    section_table = jnp.array([1.0 / 3.0, 15.0 / 16.0, 8.0 / 15.0], jnp.float32) * time_step
    selector = (jnp.arange(3, dtype=jnp.int32) == substep[0]).astype(jnp.float32)
    return jnp.sum(section_table * selector)


def on_pairs(count):
    return [(i, i ^ 1) for i in range(count)]


def first_hop(count):
    aim = {0: -4, 1: 1, 2: -1, 3: 4}
    return [(i, (i + aim[i % 4]) % count) for i in range(count)]


def second_hop(count):
    return [(i, i ^ 3 if i % 4 in (0, 3) else i) for i in range(count)]


def cell_sum(value, axis):
    count = lax.axis_size(axis)
    direct = [i for i in range(count) if i % 4 in (1, 2)]
    turning = [i for i in range(count) if i % 4 in (0, 3)]
    place = lax.axis_index(axis) % 4
    turns = (place == 0) | (place == 3)
    value = value + lax.ppermute(value, axis, [(i, i ^ 1) for i in range(count)])
    for n in range(2, count.bit_length() - 1):
        value = value + lax.ppermute(value, axis, [(i, i ^ (1 << n)) for i in direct])
    given = lax.ppermute(value, axis, [(i, i ^ 1) for i in direct])
    value = given + lax.ppermute(given, axis, [(i, i ^ 3) for i in turning])
    return jnp.where(turns, value, lax.ppermute(value, axis, [(i, i ^ 1) for i in turning]))


def wall_kernel(ids, amplitudes, edge, wall, bins):
    patches, cells = amplitudes.shape[1], ids.shape[1]
    patch = lax.broadcasted_iota(jnp.int32, (patches, cells), 0)
    hit = jnp.where(patch == ids[...], 1.0, 0.0).astype(jnp.float32)
    values = jnp.broadcast_to(amplitudes[...], (SUB, patches))
    wall[...] = lax.dot_general(
        values,
        hit,
        (((1,), (0,)), ((), ())),
        precision=lax.Precision.HIGHEST,
        preferred_element_type=jnp.float32,
    )[:1]
    bins[...] = lax.dot_general(
        edge[0],
        hit,
        (((1,), (1,)), ((), ())),
        precision=lax.Precision.HIGHEST,
        preferred_element_type=jnp.float32,
    )[SUB - 1 :]


def wall_and_bins(patch_ids, amplitudes, cotangent):
    rows, cells = cotangent.shape[1:]
    patches = amplitudes.shape[0]
    return pl.pallas_call(
        wall_kernel,
        grid=(1,),
        out_shape=(
            jax.ShapeDtypeStruct((1, cells), jnp.float32),
            jax.ShapeDtypeStruct((1, patches), jnp.float32),
        ),
        in_specs=[
            pl.BlockSpec((1, cells), lambda i: (0, 0)),
            pl.BlockSpec((1, patches), lambda i: (0, 0)),
            pl.BlockSpec((1, SUB, cells), lambda i: (0, rows // SUB - 1, 0)),
        ],
        out_specs=(
            pl.BlockSpec((1, cells), lambda i: (0, 0)),
            pl.BlockSpec((1, patches), lambda i: (0, 0)),
        ),
        compiler_params=pltpu.CompilerParams(vmem_limit_bytes=40 << 20),
    )(patch_ids, amplitudes[None], cotangent)


def local_kernel(scal, q, q_up, q_down, q_near, c, c_up, c_down, c_near, wall, coef, q_out, c_out):
    block, width = q.shape[1:]
    step, side = scal[0], scal[1]
    here, last = pl.program_id(0), pl.num_programs(0) - 1
    u, rd, ad = coef[:, 0:1], coef[:, 1:2], coef[:, 2:3]
    row = lax.broadcasted_iota(jnp.int32, (block, 1), 0)

    def around(x, up, down):
        above = jnp.where(row == 0, up, pltpu.roll(x, 1, 0))
        below = jnp.where(row == block - 1, down, pltpu.roll(x, block - 1, 0))
        return above, below

    def sides(x):
        return pltpu.roll(x, 1, 1) + pltpu.roll(x, width - 1, 1)

    x = q[0]
    first_row = pltpu.roll(x[:1], width // 2, 1)
    up = jnp.where(here == 0, first_row, q_up[0, SUB - 1 :])
    down = jnp.where(here == last, wall[...], q_down[0, :1])
    above, below = around(x, up, down)
    near = q_near[0]
    axial = near - (0.5 * side) * (near * (u + 0.5 * near)) - dissipation * x
    q_out[0] = x + step * (
        axial + rd * (above + below - 2.0 * x) + ad * (sides(x) - 2.0 * x)
    )

    y = c[0]
    weighted = rd * y
    before, after = coef_rows(coef)
    first_row = pltpu.roll(weighted[:1], width // 2, 1)
    up = jnp.where(here == 0, first_row, before * c_up[0, SUB - 1 :])
    down = jnp.where(here == last, 0.0, after * c_down[0, :1])
    above, below = around(weighted, up, down)
    axial = c_near[0] * (1.0 + (0.5 * side) * (u + x)) - dissipation * y
    c_out[0] = y + step * (
        axial + (above + below - 2.0 * weighted) + ad * (sides(y) - 2.0 * y)
    )


def coef_rows(coef):
    return coef[0:1, 3:4], coef[0:1, 4:5]


def local_parts(scal, q, q_near, c, c_near, wall, coef):
    rows, width = q.shape[1:]
    block = math.gcd(LOCAL_ROWS, rows)
    tiles, total = block // SUB, rows // SUB
    full = pl.BlockSpec((1, block, width), lambda i: (0, i, 0))
    up = pl.BlockSpec((1, SUB, width), lambda i: (0, jnp.maximum(i * tiles - 1, 0), 0))
    down = pl.BlockSpec((1, SUB, width), lambda i: (0, jnp.minimum((i + 1) * tiles, total - 1), 0))
    rd = coef[:, 1]
    before, after = jnp.roll(rd, 1), jnp.roll(rd, -block)
    coef = jnp.concatenate([coef, before[:, None], after[:, None]], axis=1)
    shape = jax.ShapeDtypeStruct(q.shape, q.dtype)
    return pl.pallas_call(
        local_kernel,
        grid=(rows // block,),
        out_shape=(shape, shape),
        in_specs=[pl.BlockSpec(memory_space=pltpu.SMEM)]
        + [full, up, down, full] * 2
        + [pl.BlockSpec((1, width), lambda i: (0, 0))]
        + [pl.BlockSpec((block, coef.shape[1]), lambda i: (i, 0))],
        out_specs=(full, full),
        compiler_params=pltpu.CompilerParams(vmem_limit_bytes=40 << 20),
        cost_estimate=pl.CostEstimate(
            flops=50 * rows * width, bytes_accessed=4 * rows * width * 6, transcendentals=0
        ),
    )(scal, q, q, q, q_near, c, c, c, c_near, wall, coef)


def state_far(scal, base, far, coef, out):
    step, side = scal[0], scal[1]
    x = far[0]
    out[0] = base[0] + step * (x + (0.5 * side) * (x * (coef[:, 0:1] + 0.5 * x)))


def cot_far(scal, base, far, state, coef, out):
    step, side = scal[0], scal[1]
    out[0] = base[0] + step * far[0] * (1.0 - (0.5 * side) * (coef[:, 0:1] + state[0]))


def add_rows(body, scal, base, part, whole, coef, start):
    rows, width = part.shape[1:]
    block = rows if rows <= ADD_ROWS else math.gcd(ADD_ROWS, rows)
    first = start // block
    full = pl.BlockSpec((1, block, width), lambda i: (0, first + i, 0))
    piece = pl.BlockSpec((1, block, width), lambda i: (0, i, 0))
    column = pl.BlockSpec((block, coef.shape[1]), lambda i: (first + i, 0))
    return pl.pallas_call(
        body,
        grid=(rows // block,),
        out_shape=jax.ShapeDtypeStruct(base.shape, base.dtype),
        in_specs=[pl.BlockSpec(memory_space=pltpu.SMEM), full, piece]
        + [full] * len(whole)
        + [column],
        out_specs=full,
        input_output_aliases={1: 0},
        compiler_params=pltpu.CompilerParams(vmem_limit_bytes=40 << 20),
        cost_estimate=pl.CostEstimate(
            flops=10 * rows * width, bytes_accessed=4 * rows * width * 4, transcendentals=0
        ),
    )(scal, base, part, *whole, coef)


def local(
    checkpoint,
    cotangent,
    amplitudes,
    patch_ids,
    substep,
    axial_speed,
    radial_diffusion,
    azimuth_diffusion,
):
    count = lax.axis_size("ax")
    rows = checkpoint.shape[1]
    patches = amplitudes.shape[0]
    assert count % 4 == 0
    one, two = first_hop(count), second_hop(count)
    cot_hop = lax.ppermute(cotangent, "ax", one)
    state_hop = lax.ppermute(checkpoint, "ax", one)
    cot_near_rows = lax.ppermute(cotangent, "ax", on_pairs(count))
    state_near_rows = lax.ppermute(checkpoint, "ax", on_pairs(count))

    wall, binned = wall_and_bins(patch_ids, amplitudes, cotangent)
    binned = lax.psum(binned, "ax") if count & (count - 1) else cell_sum(binned, "ax")

    cot_hop, binned = lax.optimization_barrier((cot_hop, binned))
    cot_far_rows = lax.ppermute(cot_hop, "ax", two)

    edges = [rows * n // STATE_PARTS for n in STATE_CUTS]
    pieces = [state_hop[:, low:high] for low, high in zip(edges, edges[1:])]

    step_size = section_size(substep)
    side = 1.0 - 2.0 * (lax.axis_index("ax") % 2).astype(jnp.float32)
    total_cells = checkpoint.shape[0] * count * checkpoint.shape[2]
    norm_factor = (patches / total_cells) ** 0.5
    gradient = (step_size * radial_diffusion[-1] * norm_factor) * binned[0]
    scal = jnp.stack([step_size, side])
    coef = jnp.stack([axial_speed, radial_diffusion, azimuth_diffusion], axis=1)

    advanced, adjoint = local_parts(
        scal, checkpoint, state_near_rows, cotangent, cot_near_rows, wall, coef
    )
    *pieces, adjoint = lax.optimization_barrier((*pieces, adjoint))
    state_far_rows = [lax.ppermute(piece, "ax", two) for piece in pieces]
    adjoint = add_rows(cot_far, scal, adjoint, cot_far_rows, [checkpoint], coef, 0)
    advanced, adjoint = lax.optimization_barrier((advanced, adjoint))
    for low, part in zip(edges, state_far_rows):
        advanced = add_rows(state_far, scal, advanced, part, [], coef, low)
    return (advanced, adjoint, gradient)


def solution(mesh):
    placed = (
        P(("case", "ax"), None, None),
        P(("case", "ax"), None, None),
        P("case"),
        P(("case", "ax"), None),
        P("case"),
        P(),
        P(),
        P(),
    )
    return jax.shard_map(
        local,
        mesh=mesh,
        in_specs=placed,
        out_specs=(P(("case", "ax"), None, None), P(("case", "ax"), None, None), P("case")),
        check_vma=False,
    )
```

```python
import math

import jax
import jax.numpy as jnp
from jax import lax
from jax.experimental import pallas as pl
from jax.experimental.pallas import tpu as pltpu
from jax.sharding import PartitionSpec as P

time_step = 0.6
dissipation = 2.0

STATE_PARTS = 48
STATE_CUTS = (0, 33, 44, 48)
LOCAL_ROWS = 64
ADD_ROWS = 88
SUB = 8


def section_size(substep):
    section_table = jnp.array([1.0 / 3.0, 15.0 / 16.0, 8.0 / 15.0], jnp.float32) * time_step
    selector = (jnp.arange(3, dtype=jnp.int32) == substep[0]).astype(jnp.float32)
    return jnp.sum(section_table * selector)


def on_pairs(count):
    return [(i, i ^ 1) for i in range(count)]


def off_pairs(count):
    return [(i, (i + 1) % count if i % 2 else (i - 1) % count) for i in range(count)]


def cell_sum(value, axis):
    count = lax.axis_size(axis)
    direct = [i for i in range(count) if i % 4 in (1, 2)]
    turning = [i for i in range(count) if i % 4 in (0, 3)]
    place = lax.axis_index(axis) % 4
    turns = (place == 0) | (place == 3)
    value = value + lax.ppermute(value, axis, [(i, i ^ 1) for i in range(count)])
    for n in range(2, count.bit_length() - 1):
        value = value + lax.ppermute(value, axis, [(i, i ^ (1 << n)) for i in direct])
    given = lax.ppermute(value, axis, [(i, i ^ 1) for i in direct])
    value = given + lax.ppermute(given, axis, [(i, i ^ 3) for i in turning])
    return jnp.where(turns, value, lax.ppermute(value, axis, [(i, i ^ 1) for i in turning]))


def wall_kernel(ids, amplitudes, edge, wall, bins):
    patches, cells = amplitudes.shape[1], ids.shape[1]
    patch = lax.broadcasted_iota(jnp.int32, (patches, cells), 0)
    hit = jnp.where(patch == ids[...], 1.0, 0.0).astype(jnp.float32)
    values = jnp.broadcast_to(amplitudes[...], (SUB, patches))
    wall[...] = lax.dot_general(
        values,
        hit,
        (((1,), (0,)), ((), ())),
        precision=lax.Precision.HIGHEST,
        preferred_element_type=jnp.float32,
    )[:1]
    bins[...] = lax.dot_general(
        edge[0],
        hit,
        (((1,), (1,)), ((), ())),
        precision=lax.Precision.HIGHEST,
        preferred_element_type=jnp.float32,
    )[SUB - 1 :]


def wall_and_bins(patch_ids, amplitudes, cotangent):
    rows, cells = cotangent.shape[1:]
    patches = amplitudes.shape[0]
    return pl.pallas_call(
        wall_kernel,
        grid=(1,),
        out_shape=(
            jax.ShapeDtypeStruct((1, cells), jnp.float32),
            jax.ShapeDtypeStruct((1, patches), jnp.float32),
        ),
        in_specs=[
            pl.BlockSpec((1, cells), lambda i: (0, 0)),
            pl.BlockSpec((1, patches), lambda i: (0, 0)),
            pl.BlockSpec((1, SUB, cells), lambda i: (0, rows // SUB - 1, 0)),
        ],
        out_specs=(
            pl.BlockSpec((1, cells), lambda i: (0, 0)),
            pl.BlockSpec((1, patches), lambda i: (0, 0)),
        ),
        compiler_params=pltpu.CompilerParams(vmem_limit_bytes=40 << 20),
    )(patch_ids, amplitudes[None], cotangent)


def local_kernel(scal, q, q_up, q_down, q_near, c, c_up, c_down, c_near, c_far, wall, coef, q_out, c_out):
    block, width = q.shape[1:]
    step, side = scal[0], scal[1]
    here, last = pl.program_id(0), pl.num_programs(0) - 1
    u, rd, ad = coef[:, 0:1], coef[:, 1:2], coef[:, 2:3]
    row = lax.broadcasted_iota(jnp.int32, (block, 1), 0)

    def around(x, up, down):
        above = jnp.where(row == 0, up, pltpu.roll(x, 1, 0))
        below = jnp.where(row == block - 1, down, pltpu.roll(x, block - 1, 0))
        return above, below

    def sides(x):
        return pltpu.roll(x, 1, 1) + pltpu.roll(x, width - 1, 1)

    x = q[0]
    first_row = pltpu.roll(x[:1], width // 2, 1)
    up = jnp.where(here == 0, first_row, q_up[0, SUB - 1 :])
    down = jnp.where(here == last, wall[...], q_down[0, :1])
    above, below = around(x, up, down)
    near = q_near[0]
    axial = near - (0.5 * side) * (near * (u + 0.5 * near)) - dissipation * x
    q_out[0] = x + step * (
        axial + rd * (above + below - 2.0 * x) + ad * (sides(x) - 2.0 * x)
    )

    y = c[0]
    weighted = rd * y
    before, after = coef_rows(coef)
    first_row = pltpu.roll(weighted[:1], width // 2, 1)
    up = jnp.where(here == 0, first_row, before * c_up[0, SUB - 1 :])
    down = jnp.where(here == last, 0.0, after * c_down[0, :1])
    above, below = around(weighted, up, down)
    slope = (0.5 * side) * (u + x)
    axial = c_near[0] * (1.0 + slope) + c_far[0] * (1.0 - slope) - dissipation * y
    c_out[0] = y + step * (
        axial + (above + below - 2.0 * weighted) + ad * (sides(y) - 2.0 * y)
    )


def coef_rows(coef):
    return coef[0:1, 3:4], coef[0:1, 4:5]


def local_parts(scal, q, q_near, c, c_near, c_far, wall, coef):
    rows, width = q.shape[1:]
    block = math.gcd(LOCAL_ROWS, rows)
    tiles, total = block // SUB, rows // SUB
    full = pl.BlockSpec((1, block, width), lambda i: (0, i, 0))
    up = pl.BlockSpec((1, SUB, width), lambda i: (0, jnp.maximum(i * tiles - 1, 0), 0))
    down = pl.BlockSpec((1, SUB, width), lambda i: (0, jnp.minimum((i + 1) * tiles, total - 1), 0))
    rd = coef[:, 1]
    before, after = jnp.roll(rd, 1), jnp.roll(rd, -block)
    coef = jnp.concatenate([coef, before[:, None], after[:, None]], axis=1)
    shape = jax.ShapeDtypeStruct(q.shape, q.dtype)
    return pl.pallas_call(
        local_kernel,
        grid=(rows // block,),
        out_shape=(shape, shape),
        in_specs=[pl.BlockSpec(memory_space=pltpu.SMEM)]
        + [full, up, down, full] * 2
        + [full]
        + [pl.BlockSpec((1, width), lambda i: (0, 0))]
        + [pl.BlockSpec((block, coef.shape[1]), lambda i: (i, 0))],
        out_specs=(full, full),
        compiler_params=pltpu.CompilerParams(vmem_limit_bytes=40 << 20),
        cost_estimate=pl.CostEstimate(
            flops=50 * rows * width, bytes_accessed=4 * rows * width * 7, transcendentals=0
        ),
    )(scal, q, q, q, q_near, c, c, c, c_near, c_far, wall, coef)


def state_far(scal, base, far, coef, out):
    step, side = scal[0], scal[1]
    x = far[0]
    out[0] = base[0] + step * (x + (0.5 * side) * (x * (coef[:, 0:1] + 0.5 * x)))


def add_rows(scal, base, part, coef, start):
    rows, width = part.shape[1:]
    whole = rows <= ADD_ROWS and start % rows == 0
    block = rows if whole else math.gcd(ADD_ROWS, rows, start)
    first = start // block
    full = pl.BlockSpec((1, block, width), lambda i: (0, first + i, 0))
    piece = pl.BlockSpec((1, block, width), lambda i: (0, i, 0))
    column = pl.BlockSpec((block, coef.shape[1]), lambda i: (first + i, 0))
    return pl.pallas_call(
        state_far,
        grid=(rows // block,),
        out_shape=jax.ShapeDtypeStruct(base.shape, base.dtype),
        in_specs=[pl.BlockSpec(memory_space=pltpu.SMEM), full, piece, column],
        out_specs=full,
        input_output_aliases={1: 0},
        compiler_params=pltpu.CompilerParams(vmem_limit_bytes=40 << 20),
        cost_estimate=pl.CostEstimate(
            flops=10 * rows * width, bytes_accessed=4 * rows * width * 3, transcendentals=0
        ),
    )(scal, base, part, coef)


def local(
    checkpoint,
    cotangent,
    amplitudes,
    patch_ids,
    substep,
    axial_speed,
    radial_diffusion,
    azimuth_diffusion,
):
    count = lax.axis_size("ax")
    rows = checkpoint.shape[1]
    patches = amplitudes.shape[0]
    near, far = on_pairs(count), off_pairs(count)
    cot_far_rows = lax.ppermute(cotangent, "ax", far)
    cot_near_rows = lax.ppermute(cotangent, "ax", near)
    state_near_rows = lax.ppermute(checkpoint, "ax", near)

    wall, binned = wall_and_bins(patch_ids, amplitudes, cotangent)
    if count & (count - 1) or count < 4:
        binned = lax.psum(binned, "ax")
    else:
        binned = cell_sum(binned, "ax")

    late, binned = lax.optimization_barrier((checkpoint, binned))
    edges = [rows * n // STATE_PARTS for n in STATE_CUTS]
    state_far_rows = [
        lax.ppermute(late[:, low:high], "ax", far) for low, high in zip(edges, edges[1:])
    ]

    step_size = section_size(substep)
    side = 1.0 - 2.0 * (lax.axis_index("ax") % 2).astype(jnp.float32)
    total_cells = checkpoint.shape[0] * count * checkpoint.shape[2]
    norm_factor = (patches / total_cells) ** 0.5
    gradient = (step_size * radial_diffusion[-1] * norm_factor) * binned[0]
    scal = jnp.stack([step_size, side])
    coef = jnp.stack([axial_speed, radial_diffusion, azimuth_diffusion], axis=1)

    cot_far_rows, cot_near_rows, state_near_rows = lax.optimization_barrier(
        (cot_far_rows, cot_near_rows, state_near_rows)
    )
    advanced, adjoint = local_parts(
        scal, checkpoint, state_near_rows, cotangent, cot_near_rows, cot_far_rows, wall, coef
    )
    for low, part in zip(edges, state_far_rows):
        advanced = add_rows(scal, advanced, part, coef, low)
    return (advanced, adjoint, gradient)


def solution(mesh):
    placed = (
        P(("case", "ax"), None, None),
        P(("case", "ax"), None, None),
        P("case"),
        P(("case", "ax"), None),
        P("case"),
        P(),
        P(),
        P(),
    )
    return jax.shard_map(
        local,
        mesh=mesh,
        in_specs=placed,
        out_specs=(P(("case", "ax"), None, None), P(("case", "ax"), None, None), P("case")),
        check_vma=False,
    )
```

```python
import math

import jax
import jax.numpy as jnp
from jax import lax
from jax.experimental import pallas as pl
from jax.experimental.pallas import tpu as pltpu
from jax.sharding import PartitionSpec as P

time_step = 0.6
dissipation = 2.0

STATE_PARTS = 48
STATE_CUTS = (0, 33, 44, 48)
LOCAL_ROWS = 64
ADD_ROWS = 88
SUB = 8


def section_size(substep):
    section_table = jnp.array([1.0 / 3.0, 15.0 / 16.0, 8.0 / 15.0], jnp.float32) * time_step
    selector = (jnp.arange(3, dtype=jnp.int32) == substep[0]).astype(jnp.float32)
    return jnp.sum(section_table * selector)


def on_pairs(count):
    return [(i, i ^ 1) for i in range(count)]


def off_pairs(count):
    return [(i, (i + 1) % count if i % 2 else (i - 1) % count) for i in range(count)]


def cell_sum(value, axis):
    count = lax.axis_size(axis)
    direct = [i for i in range(count) if i % 4 in (1, 2)]
    turning = [i for i in range(count) if i % 4 in (0, 3)]
    place = lax.axis_index(axis) % 4
    turns = (place == 0) | (place == 3)
    value = value + lax.ppermute(value, axis, [(i, i ^ 1) for i in range(count)])
    for n in range(2, count.bit_length() - 1):
        value = value + lax.ppermute(value, axis, [(i, i ^ (1 << n)) for i in direct])
    given = lax.ppermute(value, axis, [(i, i ^ 1) for i in direct])
    value = given + lax.ppermute(given, axis, [(i, i ^ 3) for i in turning])
    return jnp.where(turns, value, lax.ppermute(value, axis, [(i, i ^ 1) for i in turning]))


def wall_kernel(ids, amplitudes, edge, wall, bins):
    patches, cells = amplitudes.shape[1], ids.shape[1]
    patch = lax.broadcasted_iota(jnp.int32, (patches, cells), 0)
    hit = jnp.where(patch == ids[...], 1.0, 0.0).astype(jnp.float32)
    values = jnp.broadcast_to(amplitudes[...], (SUB, patches))
    wall[...] = lax.dot_general(
        values,
        hit,
        (((1,), (0,)), ((), ())),
        precision=lax.Precision.HIGHEST,
        preferred_element_type=jnp.float32,
    )[:1]
    bins[...] = lax.dot_general(
        edge[0],
        hit,
        (((1,), (1,)), ((), ())),
        precision=lax.Precision.HIGHEST,
        preferred_element_type=jnp.float32,
    )[SUB - 1 :]


def wall_and_bins(patch_ids, amplitudes, cotangent):
    rows, cells = cotangent.shape[1:]
    patches = amplitudes.shape[0]
    return pl.pallas_call(
        wall_kernel,
        grid=(1,),
        out_shape=(
            jax.ShapeDtypeStruct((1, cells), jnp.float32),
            jax.ShapeDtypeStruct((1, patches), jnp.float32),
        ),
        in_specs=[
            pl.BlockSpec((1, cells), lambda i: (0, 0)),
            pl.BlockSpec((1, patches), lambda i: (0, 0)),
            pl.BlockSpec((1, SUB, cells), lambda i: (0, rows // SUB - 1, 0)),
        ],
        out_specs=(
            pl.BlockSpec((1, cells), lambda i: (0, 0)),
            pl.BlockSpec((1, patches), lambda i: (0, 0)),
        ),
        compiler_params=pltpu.CompilerParams(vmem_limit_bytes=40 << 20),
    )(patch_ids, amplitudes[None], cotangent)


def local_kernel(scal, q, q_up, q_down, q_near, c, c_up, c_down, c_near, c_far, wall, coef, q_out, c_out):
    block, width = q.shape[1:]
    step, side = scal[0], scal[1]
    here, last = pl.program_id(0), pl.num_programs(0) - 1
    u, rd, ad = coef[:, 0:1], coef[:, 1:2], coef[:, 2:3]
    row = lax.broadcasted_iota(jnp.int32, (block, 1), 0)

    def around(x, up, down):
        above = jnp.where(row == 0, up, pltpu.roll(x, 1, 0))
        below = jnp.where(row == block - 1, down, pltpu.roll(x, block - 1, 0))
        return above, below

    def sides(x):
        return pltpu.roll(x, 1, 1) + pltpu.roll(x, width - 1, 1)

    x = q[0]
    first_row = pltpu.roll(x[:1], width // 2, 1)
    up = jnp.where(here == 0, first_row, q_up[0, SUB - 1 :])
    down = jnp.where(here == last, wall[...], q_down[0, :1])
    above, below = around(x, up, down)
    near = q_near[0]
    axial = near - (0.5 * side) * (near * (u + 0.5 * near)) - dissipation * x
    q_out[0] = x + step * (
        axial + rd * (above + below - 2.0 * x) + ad * (sides(x) - 2.0 * x)
    )

    y = c[0]
    weighted = rd * y
    before, after = coef_rows(coef)
    first_row = pltpu.roll(weighted[:1], width // 2, 1)
    up = jnp.where(here == 0, first_row, before * c_up[0, SUB - 1 :])
    down = jnp.where(here == last, 0.0, after * c_down[0, :1])
    above, below = around(weighted, up, down)
    slope = (0.5 * side) * (u + x)
    axial = c_near[0] * (1.0 + slope) + c_far[0] * (1.0 - slope) - dissipation * y
    c_out[0] = y + step * (
        axial + (above + below - 2.0 * weighted) + ad * (sides(y) - 2.0 * y)
    )


def coef_rows(coef):
    return coef[0:1, 3:4], coef[0:1, 4:5]


def local_parts(scal, q, q_near, c, c_near, c_far, wall, coef):
    rows, width = q.shape[1:]
    block = math.gcd(LOCAL_ROWS, rows)
    tiles, total = block // SUB, rows // SUB
    full = pl.BlockSpec((1, block, width), lambda i: (0, i, 0))
    up = pl.BlockSpec((1, SUB, width), lambda i: (0, jnp.maximum(i * tiles - 1, 0), 0))
    down = pl.BlockSpec((1, SUB, width), lambda i: (0, jnp.minimum((i + 1) * tiles, total - 1), 0))
    rd = coef[:, 1]
    before, after = jnp.roll(rd, 1), jnp.roll(rd, -block)
    coef = jnp.concatenate([coef, before[:, None], after[:, None]], axis=1)
    shape = jax.ShapeDtypeStruct(q.shape, q.dtype)
    return pl.pallas_call(
        local_kernel,
        grid=(rows // block,),
        out_shape=(shape, shape),
        in_specs=[pl.BlockSpec(memory_space=pltpu.SMEM)]
        + [full, up, down, full] * 2
        + [full]
        + [pl.BlockSpec((1, width), lambda i: (0, 0))]
        + [pl.BlockSpec((block, coef.shape[1]), lambda i: (i, 0))],
        out_specs=(full, full),
        compiler_params=pltpu.CompilerParams(vmem_limit_bytes=40 << 20),
        cost_estimate=pl.CostEstimate(
            flops=50 * rows * width, bytes_accessed=4 * rows * width * 7, transcendentals=0
        ),
    )(scal, q, q, q, q_near, c, c, c, c_near, c_far, wall, coef)


def state_far(base, far, weight, out):
    x = far[0]
    out[0] = base[0] + x * (weight[:, 0:1] + weight[:, 1:2] * x)


def add_rows(base, part, weight, start):
    rows, width = part.shape[1:]
    whole = rows <= ADD_ROWS and start % rows == 0
    block = rows if whole else math.gcd(ADD_ROWS, rows, start)
    first = start // block
    full = pl.BlockSpec((1, block, width), lambda i: (0, first + i, 0))
    piece = pl.BlockSpec((1, block, width), lambda i: (0, i, 0))
    column = pl.BlockSpec((block, weight.shape[1]), lambda i: (first + i, 0))
    return pl.pallas_call(
        state_far,
        grid=(rows // block,),
        out_shape=jax.ShapeDtypeStruct(base.shape, base.dtype),
        in_specs=[full, piece, column],
        out_specs=full,
        input_output_aliases={0: 0},
        compiler_params=pltpu.CompilerParams(vmem_limit_bytes=40 << 20),
        cost_estimate=pl.CostEstimate(
            flops=10 * rows * width, bytes_accessed=4 * rows * width * 3, transcendentals=0
        ),
    )(base, part, weight)


def last_rows(base, part, weight):
    rows, width = part.shape[1:]
    start = base.shape[1] - rows

    def kernel(base, far, weight, out, have, x, w, sems):
        here = pl.ds(start, rows)
        copies = [
            pltpu.make_async_copy(base.at[0, here], have, sems.at[0]),
            pltpu.make_async_copy(far.at[0], x, sems.at[1]),
            pltpu.make_async_copy(weight.at[here], w, sems.at[2]),
        ]
        for copy in copies:
            copy.start()
        for copy in copies:
            copy.wait()
        have[...] = have[...] + x[...] * (w[:, 0:1] + w[:, 1:2] * x[...])
        back = pltpu.make_async_copy(have, out.at[0, here], sems.at[3])
        back.start()
        back.wait()

    anywhere = pl.BlockSpec(memory_space=pl.ANY)
    return pl.pallas_call(
        kernel,
        out_shape=jax.ShapeDtypeStruct(base.shape, base.dtype),
        in_specs=[anywhere] * 3,
        out_specs=anywhere,
        scratch_shapes=[
            pltpu.VMEM((rows, width), jnp.float32),
            pltpu.VMEM((rows, width), jnp.float32),
            pltpu.VMEM((rows, weight.shape[1]), jnp.float32),
            pltpu.SemaphoreType.DMA((4,)),
        ],
        input_output_aliases={0: 0},
        compiler_params=pltpu.CompilerParams(vmem_limit_bytes=40 << 20),
        cost_estimate=pl.CostEstimate(
            flops=10 * rows * width, bytes_accessed=4 * rows * width * 3, transcendentals=0
        ),
    )(base, part, weight)


def local(
    checkpoint,
    cotangent,
    amplitudes,
    patch_ids,
    substep,
    axial_speed,
    radial_diffusion,
    azimuth_diffusion,
):
    count = lax.axis_size("ax")
    rows = checkpoint.shape[1]
    patches = amplitudes.shape[0]
    near, far = on_pairs(count), off_pairs(count)
    cot_far_rows = lax.ppermute(cotangent, "ax", far)
    cot_near_rows = lax.ppermute(cotangent, "ax", near)
    state_near_rows = lax.ppermute(checkpoint, "ax", near)

    wall, binned = wall_and_bins(patch_ids, amplitudes, cotangent)
    if count & (count - 1) or count < 4:
        binned = lax.psum(binned, "ax")
    else:
        binned = cell_sum(binned, "ax")

    late, binned = lax.optimization_barrier((checkpoint, binned))
    edges = [rows * n // STATE_PARTS for n in STATE_CUTS]
    state_far_rows = [
        lax.ppermute(late[:, low:high], "ax", far) for low, high in zip(edges, edges[1:])
    ]

    step_size = section_size(substep)
    side = 1.0 - 2.0 * (lax.axis_index("ax") % 2).astype(jnp.float32)
    total_cells = checkpoint.shape[0] * count * checkpoint.shape[2]
    norm_factor = (patches / total_cells) ** 0.5
    gradient = (step_size * radial_diffusion[-1] * norm_factor) * binned[0]
    scal = jnp.stack([step_size, side])
    coef = jnp.stack([axial_speed, radial_diffusion, azimuth_diffusion], axis=1)
    half = 0.5 * side * step_size
    weight = jnp.stack(
        [step_size + half * axial_speed, jnp.broadcast_to(0.5 * half, axial_speed.shape)], axis=1
    )

    cot_far_rows, cot_near_rows, state_near_rows = lax.optimization_barrier(
        (cot_far_rows, cot_near_rows, state_near_rows)
    )
    advanced, adjoint = local_parts(
        scal, checkpoint, state_near_rows, cotangent, cot_near_rows, cot_far_rows, wall, coef
    )
    for low, part in zip(edges, state_far_rows[:-1]):
        advanced = add_rows(advanced, part, weight, low)
    advanced = last_rows(advanced, state_far_rows[-1], weight)
    return (advanced, adjoint, gradient)


def solution(mesh):
    placed = (
        P(("case", "ax"), None, None),
        P(("case", "ax"), None, None),
        P("case"),
        P(("case", "ax"), None),
        P("case"),
        P(),
        P(),
        P(),
    )
    return jax.shard_map(
        local,
        mesh=mesh,
        in_specs=placed,
        out_specs=(P(("case", "ax"), None, None), P(("case", "ax"), None, None), P("case")),
        check_vma=False,
    )
```

```python
import math

import jax
import jax.numpy as jnp
from jax import lax
from jax.experimental import pallas as pl
from jax.experimental.pallas import tpu as pltpu
from jax.sharding import PartitionSpec as P

time_step = 0.6
dissipation = 2.0

STATE_PARTS = 48
STATE_CUTS = (0, 33, 44, 48)
LOCAL_ROWS = 64
ADD_ROWS = 88
SUB = 8


def section_size(substep):
    section_table = jnp.array([1.0 / 3.0, 15.0 / 16.0, 8.0 / 15.0], jnp.float32) * time_step
    selector = (jnp.arange(3, dtype=jnp.int32) == substep[0]).astype(jnp.float32)
    return jnp.sum(section_table * selector)


def on_pairs(count):
    return [(i, i ^ 1) for i in range(count)]


def off_pairs(count):
    return [(i, (i + 1) % count if i % 2 else (i - 1) % count) for i in range(count)]


def cell_sum(value, axis):
    count = lax.axis_size(axis)
    direct = [i for i in range(count) if i % 4 in (1, 2)]
    turning = [i for i in range(count) if i % 4 in (0, 3)]
    place = lax.axis_index(axis) % 4
    turns = (place == 0) | (place == 3)
    value = value + lax.ppermute(value, axis, [(i, i ^ 1) for i in range(count)])
    for n in range(2, count.bit_length() - 1):
        value = value + lax.ppermute(value, axis, [(i, i ^ (1 << n)) for i in direct])
    given = lax.ppermute(value, axis, [(i, i ^ 1) for i in direct])
    value = given + lax.ppermute(given, axis, [(i, i ^ 3) for i in turning])
    return jnp.where(turns, value, lax.ppermute(value, axis, [(i, i ^ 1) for i in turning]))


def wall_kernel(ids, amplitudes, edge, wall, bins):
    patches, cells = amplitudes.shape[1], ids.shape[1]
    patch = lax.broadcasted_iota(jnp.int32, (patches, cells), 0)
    hit = jnp.where(patch == ids[...], 1.0, 0.0).astype(jnp.float32)
    values = jnp.broadcast_to(amplitudes[...], (SUB, patches))
    wall[...] = lax.dot_general(
        values,
        hit,
        (((1,), (0,)), ((), ())),
        precision=lax.Precision.HIGHEST,
        preferred_element_type=jnp.float32,
    )[:1]
    bins[...] = lax.dot_general(
        edge[0],
        hit,
        (((1,), (1,)), ((), ())),
        precision=lax.Precision.HIGHEST,
        preferred_element_type=jnp.float32,
    )[SUB - 1 :]


def wall_and_bins(patch_ids, amplitudes, cotangent):
    rows, cells = cotangent.shape[1:]
    patches = amplitudes.shape[0]
    return pl.pallas_call(
        wall_kernel,
        grid=(1,),
        out_shape=(
            jax.ShapeDtypeStruct((1, cells), jnp.float32),
            jax.ShapeDtypeStruct((1, patches), jnp.float32),
        ),
        in_specs=[
            pl.BlockSpec((1, cells), lambda i: (0, 0)),
            pl.BlockSpec((1, patches), lambda i: (0, 0)),
            pl.BlockSpec((1, SUB, cells), lambda i: (0, rows // SUB - 1, 0)),
        ],
        out_specs=(
            pl.BlockSpec((1, cells), lambda i: (0, 0)),
            pl.BlockSpec((1, patches), lambda i: (0, 0)),
        ),
        compiler_params=pltpu.CompilerParams(vmem_limit_bytes=40 << 20),
    )(patch_ids, amplitudes[None], cotangent)


def local_kernel(scal, q, q_up, q_down, q_near, c, c_up, c_down, c_near, c_far, wall, coef, q_out, c_out):
    block, width = q.shape[1:]
    step, side = scal[0], scal[1]
    here, last = pl.program_id(0), pl.num_programs(0) - 1
    u, rd, ad = coef[:, 0:1], coef[:, 1:2], coef[:, 2:3]
    row = lax.broadcasted_iota(jnp.int32, (block, 1), 0)

    def around(x, up, down):
        above = jnp.where(row == 0, up, pltpu.roll(x, 1, 0))
        below = jnp.where(row == block - 1, down, pltpu.roll(x, block - 1, 0))
        return above, below

    def sides(x):
        return pltpu.roll(x, 1, 1) + pltpu.roll(x, width - 1, 1)

    x = q[0]
    first_row = pltpu.roll(x[:1], width // 2, 1)
    up = jnp.where(here == 0, first_row, q_up[0, SUB - 1 :])
    down = jnp.where(here == last, wall[...], q_down[0, :1])
    above, below = around(x, up, down)
    near = q_near[0]
    axial = near - (0.5 * side) * (near * (u + 0.5 * near)) - dissipation * x
    q_out[0] = x + step * (
        axial + rd * (above + below - 2.0 * x) + ad * (sides(x) - 2.0 * x)
    )

    y = c[0]
    weighted = rd * y
    before, after = coef_rows(coef)
    first_row = pltpu.roll(weighted[:1], width // 2, 1)
    up = jnp.where(here == 0, first_row, before * c_up[0, SUB - 1 :])
    down = jnp.where(here == last, 0.0, after * c_down[0, :1])
    above, below = around(weighted, up, down)
    slope = (0.5 * side) * (u + x)
    axial = c_near[0] * (1.0 + slope) + c_far[0] * (1.0 - slope) - dissipation * y
    c_out[0] = y + step * (
        axial + (above + below - 2.0 * weighted) + ad * (sides(y) - 2.0 * y)
    )


def coef_rows(coef):
    return coef[0:1, 3:4], coef[0:1, 4:5]


def local_parts(scal, q, q_near, c, c_near, c_far, wall, coef):
    rows, width = q.shape[1:]
    block = math.gcd(LOCAL_ROWS, rows)
    tiles, total = block // SUB, rows // SUB
    full = pl.BlockSpec((1, block, width), lambda i: (0, i, 0))
    up = pl.BlockSpec((1, SUB, width), lambda i: (0, jnp.maximum(i * tiles - 1, 0), 0))
    down = pl.BlockSpec((1, SUB, width), lambda i: (0, jnp.minimum((i + 1) * tiles, total - 1), 0))
    rd = coef[:, 1]
    before, after = jnp.roll(rd, 1), jnp.roll(rd, -block)
    coef = jnp.concatenate([coef, before[:, None], after[:, None]], axis=1)
    shape = jax.ShapeDtypeStruct(q.shape, q.dtype)
    return pl.pallas_call(
        local_kernel,
        grid=(rows // block,),
        out_shape=(shape, shape),
        in_specs=[pl.BlockSpec(memory_space=pltpu.SMEM)]
        + [full, up, down, full] * 2
        + [full]
        + [pl.BlockSpec((1, width), lambda i: (0, 0))]
        + [pl.BlockSpec((block, coef.shape[1]), lambda i: (i, 0))],
        out_specs=(full, full),
        compiler_params=pltpu.CompilerParams(vmem_limit_bytes=40 << 20),
        cost_estimate=pl.CostEstimate(
            flops=50 * rows * width, bytes_accessed=4 * rows * width * 7, transcendentals=0
        ),
    )(scal, q, q, q, q_near, c, c, c, c_near, c_far, wall, coef)


def state_far(base, far, weight, out):
    x = far[0]
    out[0] = base[0] + x * (weight[:, 0:1] + weight[:, 1:2] * x)


def add_rows(base, part, weight, start):
    rows, width = part.shape[1:]
    whole = rows <= ADD_ROWS and start % rows == 0
    block = rows if whole else math.gcd(ADD_ROWS, rows, start)
    first = start // block
    full = pl.BlockSpec((1, block, width), lambda i: (0, first + i, 0))
    piece = pl.BlockSpec((1, block, width), lambda i: (0, i, 0))
    column = pl.BlockSpec((block, weight.shape[1]), lambda i: (first + i, 0))
    return pl.pallas_call(
        state_far,
        grid=(rows // block,),
        out_shape=jax.ShapeDtypeStruct(base.shape, base.dtype),
        in_specs=[full, piece, column],
        out_specs=full,
        input_output_aliases={0: 0},
        compiler_params=pltpu.CompilerParams(vmem_limit_bytes=40 << 20),
        cost_estimate=pl.CostEstimate(
            flops=10 * rows * width, bytes_accessed=4 * rows * width * 3, transcendentals=0
        ),
    )(base, part, weight)


def put_rows(out, base, part, weight, start):
    rows, width = part.shape[1:]

    def kernel(base, far, weight, before, out, fresh, sem):
        x = far[0]
        of_row = weight[pl.ds(start, rows), :]
        fresh[...] = base[0] + x * (of_row[:, 0:1] + of_row[:, 1:2] * x)
        store = pltpu.make_async_copy(fresh, out.at[0, pl.ds(start, rows)], sem)
        store.start()
        store.wait()

    anywhere = pl.BlockSpec(memory_space=pl.ANY)
    return pl.pallas_call(
        kernel,
        out_shape=jax.ShapeDtypeStruct(out.shape, out.dtype),
        in_specs=[pl.BlockSpec(memory_space=pltpu.VMEM)] * 3 + [anywhere],
        out_specs=anywhere,
        scratch_shapes=[pltpu.VMEM((rows, width), jnp.float32), pltpu.SemaphoreType.DMA],
        input_output_aliases={3: 0},
        compiler_params=pltpu.CompilerParams(vmem_limit_bytes=40 << 20),
        cost_estimate=pl.CostEstimate(
            flops=10 * rows * width, bytes_accessed=4 * rows * width * 3, transcendentals=0
        ),
    )(base, part, weight, out)


def local(
    checkpoint,
    cotangent,
    amplitudes,
    patch_ids,
    substep,
    axial_speed,
    radial_diffusion,
    azimuth_diffusion,
):
    count = lax.axis_size("ax")
    rows = checkpoint.shape[1]
    patches = amplitudes.shape[0]
    near, far = on_pairs(count), off_pairs(count)
    cot_far_rows = lax.ppermute(cotangent, "ax", far)
    cot_near_rows = lax.ppermute(cotangent, "ax", near)
    state_near_rows = lax.ppermute(checkpoint, "ax", near)

    wall, binned = wall_and_bins(patch_ids, amplitudes, cotangent)
    if count & (count - 1) or count < 4:
        binned = lax.psum(binned, "ax")
    else:
        binned = cell_sum(binned, "ax")

    late, binned = lax.optimization_barrier((checkpoint, binned))
    edges = [rows * n // STATE_PARTS for n in STATE_CUTS]
    state_far_rows = [
        lax.ppermute(late[:, low:high], "ax", far) for low, high in zip(edges, edges[1:])
    ]

    step_size = section_size(substep)
    side = 1.0 - 2.0 * (lax.axis_index("ax") % 2).astype(jnp.float32)
    total_cells = checkpoint.shape[0] * count * checkpoint.shape[2]
    norm_factor = (patches / total_cells) ** 0.5
    gradient = (step_size * radial_diffusion[-1] * norm_factor) * binned[0]
    scal = jnp.stack([step_size, side])
    coef = jnp.stack([axial_speed, radial_diffusion, azimuth_diffusion], axis=1)
    half = 0.5 * side * step_size
    weight = jnp.stack(
        [step_size + half * axial_speed, jnp.broadcast_to(0.5 * half, axial_speed.shape)], axis=1
    )

    cot_far_rows, cot_near_rows, state_near_rows = lax.optimization_barrier(
        (cot_far_rows, cot_near_rows, state_near_rows)
    )
    advanced, adjoint = local_parts(
        scal, checkpoint, state_near_rows, cotangent, cot_near_rows, cot_far_rows, wall, coef
    )
    bases = [advanced[:, low:high] for low, high in zip(edges[1:], edges[2:])]
    advanced, *bases = lax.optimization_barrier((advanced, *bases))
    advanced = add_rows(advanced, state_far_rows[0], weight, 0)
    for low, base, part in zip(edges[1:], bases, state_far_rows[1:]):
        advanced = put_rows(advanced, base, part, weight, low)
    return (advanced, adjoint, gradient)


def solution(mesh):
    placed = (
        P(("case", "ax"), None, None),
        P(("case", "ax"), None, None),
        P("case"),
        P(("case", "ax"), None),
        P("case"),
        P(),
        P(),
        P(),
    )
    return jax.shard_map(
        local,
        mesh=mesh,
        in_specs=placed,
        out_specs=(P(("case", "ax"), None, None), P(("case", "ax"), None, None), P("case")),
        check_vma=False,
    )
```

```python
import math

import jax
import jax.numpy as jnp
from jax import lax
from jax.experimental import pallas as pl
from jax.experimental.pallas import tpu as pltpu
from jax.sharding import PartitionSpec as P

time_step = 0.6
dissipation = 2.0

STATE_PARTS = 48
STATE_CUTS = (0, 33, 44, 48)
LOCAL_ROWS = 96
FAR_WEIGHT = 100000
ADD_ROWS = 88
SUB = 8


def section_size(substep):
    section_table = jnp.array([1.0 / 3.0, 15.0 / 16.0, 8.0 / 15.0], jnp.float32) * time_step
    selector = (jnp.arange(3, dtype=jnp.int32) == substep[0]).astype(jnp.float32)
    return jnp.sum(section_table * selector)


def on_pairs(count):
    return [(i, i ^ 1) for i in range(count)]


def off_pairs(count):
    return [(i, (i + 1) % count if i % 2 else (i - 1) % count) for i in range(count)]


def cell_sum(value, axis):
    count = lax.axis_size(axis)
    direct = [i for i in range(count) if i % 4 in (1, 2)]
    turning = [i for i in range(count) if i % 4 in (0, 3)]
    place = lax.axis_index(axis) % 4
    turns = (place == 0) | (place == 3)
    value = value + lax.ppermute(value, axis, [(i, i ^ 1) for i in range(count)])
    for n in range(2, count.bit_length() - 1):
        value = value + lax.ppermute(value, axis, [(i, i ^ (1 << n)) for i in direct])
    given = lax.ppermute(value, axis, [(i, i ^ 1) for i in direct])
    value = given + lax.ppermute(given, axis, [(i, i ^ 3) for i in turning])
    return jnp.where(turns, value, lax.ppermute(value, axis, [(i, i ^ 1) for i in turning]))


def wall_kernel(ids, amplitudes, edge, wall, bins):
    patches, cells = amplitudes.shape[1], ids.shape[1]
    patch = lax.broadcasted_iota(jnp.int32, (patches, cells), 0)
    hit = jnp.where(patch == ids[...], 1.0, 0.0).astype(jnp.float32)
    values = jnp.broadcast_to(amplitudes[...], (SUB, patches))
    wall[...] = lax.dot_general(
        values,
        hit,
        (((1,), (0,)), ((), ())),
        precision=lax.Precision.HIGHEST,
        preferred_element_type=jnp.float32,
    )[:1]
    bins[...] = lax.dot_general(
        edge[0],
        hit,
        (((1,), (1,)), ((), ())),
        precision=lax.Precision.HIGHEST,
        preferred_element_type=jnp.float32,
    )[SUB - 1 :]


def wall_and_bins(patch_ids, amplitudes, cotangent):
    rows, cells = cotangent.shape[1:]
    patches = amplitudes.shape[0]
    return pl.pallas_call(
        wall_kernel,
        grid=(1,),
        out_shape=(
            jax.ShapeDtypeStruct((1, cells), jnp.float32),
            jax.ShapeDtypeStruct((1, patches), jnp.float32),
        ),
        in_specs=[
            pl.BlockSpec((1, cells), lambda i: (0, 0)),
            pl.BlockSpec((1, patches), lambda i: (0, 0)),
            pl.BlockSpec((1, SUB, cells), lambda i: (0, rows // SUB - 1, 0)),
        ],
        out_specs=(
            pl.BlockSpec((1, cells), lambda i: (0, 0)),
            pl.BlockSpec((1, patches), lambda i: (0, 0)),
        ),
        compiler_params=pltpu.CompilerParams(vmem_limit_bytes=40 << 20),
    )(patch_ids, amplitudes[None], cotangent)


def local_kernel(scal, q, q_up, q_down, q_one, q_two, c, c_up, c_down, c_one, c_two, far, wall, coef, q_out, c_out):
    block, width = q.shape[1:]
    step, side = scal[0], scal[1]
    here, last = pl.program_id(0), pl.num_programs(0) - 1
    u, rd, ad = coef[:, 0:1], coef[:, 1:2], coef[:, 2:3]
    row = lax.broadcasted_iota(jnp.int32, (block, 1), 0)

    def around(x, up, down):
        above = jnp.where(row == 0, up, pltpu.roll(x, 1, 0))
        below = jnp.where(row == block - 1, down, pltpu.roll(x, block - 1, 0))
        return above, below

    def sides(x):
        return pltpu.roll(x, 1, 1) + pltpu.roll(x, width - 1, 1)

    x = q[0]
    first_row = pltpu.roll(x[:1], width // 2, 1)
    up = jnp.where(here == 0, first_row, q_up[0, SUB - 1 :])
    down = jnp.where(here == last, wall[...], q_down[0, :1])
    above, below = around(x, up, down)
    near = q_one[0] + q_two[0]
    axial = near - (0.5 * side) * (near * (u + 0.5 * near)) - dissipation * x
    q_out[0] = x + step * (
        axial + rd * (above + below - 2.0 * x) + ad * (sides(x) - 2.0 * x)
    )

    y = c[0]
    weighted = rd * y
    before, after = coef_rows(coef)
    first_row = pltpu.roll(weighted[:1], width // 2, 1)
    up = jnp.where(here == 0, first_row, before * c_up[0, SUB - 1 :])
    down = jnp.where(here == last, 0.0, after * c_down[0, :1])
    above, below = around(weighted, up, down)
    slope = (0.5 * side) * (u + x)
    axial = (c_one[0] + c_two[0]) * (1.0 + slope) - dissipation * y
    c_out[0] = y + far[0] + step * (
        axial + (above + below - 2.0 * weighted) + ad * (sides(y) - 2.0 * y)
    )


def coef_rows(coef):
    return coef[0:1, 3:4], coef[0:1, 4:5]


def local_parts(scal, q, q_near, c, c_near, far, wall, coef):
    rows, width = q.shape[1:]
    block = math.gcd(LOCAL_ROWS, rows)
    tiles, total = block // SUB, rows // SUB
    full = pl.BlockSpec((1, block, width), lambda i: (0, i, 0))
    up = pl.BlockSpec((1, SUB, width), lambda i: (0, jnp.maximum(i * tiles - 1, 0), 0))
    down = pl.BlockSpec((1, SUB, width), lambda i: (0, jnp.minimum((i + 1) * tiles, total - 1), 0))
    rd = coef[:, 1]
    before, after = jnp.roll(rd, 1), jnp.roll(rd, -block)
    coef = jnp.concatenate([coef, before[:, None], after[:, None]], axis=1)
    shape = jax.ShapeDtypeStruct(q.shape, q.dtype)
    return pl.pallas_call(
        local_kernel,
        grid=(rows // block,),
        out_shape=(shape, shape),
        in_specs=[pl.BlockSpec(memory_space=pltpu.SMEM)]
        + [full, up, down, full, full] * 2
        + [full]
        + [pl.BlockSpec((1, width), lambda i: (0, 0))]
        + [pl.BlockSpec((block, coef.shape[1]), lambda i: (i, 0))],
        out_specs=(full, full),
        compiler_params=pltpu.CompilerParams(vmem_limit_bytes=40 << 20),
        cost_estimate=pl.CostEstimate(
            flops=50 * rows * width, bytes_accessed=4 * rows * width * 7, transcendentals=0
        ),
    )(scal, q, q, q, *q_near, c, c, c, *c_near, far, wall, coef)


def cot_kernel(scal, far, state, coef, out):
    out[0] = scal[0] * far[0] * (1.0 - (0.5 * scal[1]) * (coef[:, 0:1] + state[0]))


def cot_term(scal, far, state, coef):
    rows, width = far.shape[1:]
    block = math.gcd(128, rows)
    full = pl.BlockSpec((1, block, width), lambda i: (0, i, 0))
    return pl.pallas_call(
        cot_kernel,
        grid=(rows // block,),
        out_shape=jax.ShapeDtypeStruct(far.shape, far.dtype),
        in_specs=[pl.BlockSpec(memory_space=pltpu.SMEM), full, full]
        + [pl.BlockSpec((block, coef.shape[1]), lambda i: (i, 0))],
        out_specs=full,
        compiler_params=pltpu.CompilerParams(vmem_limit_bytes=40 << 20),
        cost_estimate=pl.CostEstimate(
            flops=FAR_WEIGHT * rows * width, bytes_accessed=4 * rows * width * 3, transcendentals=0
        ),
    )(scal, far, state, coef)


def state_far(base, far, weight, out):
    x = far[0]
    out[0] = base[0] + x * (weight[:, 0:1] + weight[:, 1:2] * x)


def add_rows(base, part, weight, start):
    rows, width = part.shape[1:]
    whole = rows <= ADD_ROWS and start % rows == 0
    block = rows if whole else math.gcd(ADD_ROWS, rows, start)
    first = start // block
    full = pl.BlockSpec((1, block, width), lambda i: (0, first + i, 0))
    piece = pl.BlockSpec((1, block, width), lambda i: (0, i, 0))
    column = pl.BlockSpec((block, weight.shape[1]), lambda i: (first + i, 0))
    return pl.pallas_call(
        state_far,
        grid=(rows // block,),
        out_shape=jax.ShapeDtypeStruct(base.shape, base.dtype),
        in_specs=[full, piece, column],
        out_specs=full,
        input_output_aliases={0: 0},
        compiler_params=pltpu.CompilerParams(vmem_limit_bytes=40 << 20),
        cost_estimate=pl.CostEstimate(
            flops=10 * rows * width, bytes_accessed=4 * rows * width * 3, transcendentals=0
        ),
    )(base, part, weight)


def put_rows(out, base, part, weight, start):
    rows, width = part.shape[1:]

    def kernel(base, far, weight, before, out, fresh, sem):
        x = far[0]
        of_row = weight[pl.ds(start, rows), :]
        fresh[...] = base[0] + x * (of_row[:, 0:1] + of_row[:, 1:2] * x)
        store = pltpu.make_async_copy(fresh, out.at[0, pl.ds(start, rows)], sem)
        store.start()
        store.wait()

    anywhere = pl.BlockSpec(memory_space=pl.ANY)
    return pl.pallas_call(
        kernel,
        out_shape=jax.ShapeDtypeStruct(out.shape, out.dtype),
        in_specs=[pl.BlockSpec(memory_space=pltpu.VMEM)] * 3 + [anywhere],
        out_specs=anywhere,
        scratch_shapes=[pltpu.VMEM((rows, width), jnp.float32), pltpu.SemaphoreType.DMA],
        input_output_aliases={3: 0},
        compiler_params=pltpu.CompilerParams(vmem_limit_bytes=40 << 20),
        cost_estimate=pl.CostEstimate(
            flops=10 * rows * width, bytes_accessed=4 * rows * width * 3, transcendentals=0
        ),
    )(base, part, weight, out)


def local(
    checkpoint,
    cotangent,
    amplitudes,
    patch_ids,
    substep,
    axial_speed,
    radial_diffusion,
    azimuth_diffusion,
):
    count = lax.axis_size("ax")
    rows = checkpoint.shape[1]
    patches = amplitudes.shape[0]
    far = off_pairs(count)
    toward = [(i, i ^ 1) for i in range(count) if i % 4 in (1, 2)]
    back = [(i, i ^ 1) for i in range(count) if i % 4 not in (1, 2)]
    cot_far_rows = lax.ppermute(cotangent, "ax", far)
    cot_near = [lax.ppermute(cotangent, "ax", toward)]
    state_near = [lax.ppermute(checkpoint, "ax", toward)]

    wall, binned = wall_and_bins(patch_ids, amplitudes, cotangent)
    if count & (count - 1) or count < 4:
        binned = lax.psum(binned, "ax")
    else:
        binned = cell_sum(binned, "ax")

    late, cot_late, binned, *first = lax.optimization_barrier(
        (checkpoint, cotangent, binned, *cot_near, *state_near)
    )
    cot_near = [first[0], lax.ppermute(cot_late, "ax", back)]
    state_near = [first[1], lax.ppermute(late, "ax", back)]
    edges = [rows * n // STATE_PARTS for n in STATE_CUTS]
    state_far_rows = [
        lax.ppermute(late[:, low:high], "ax", far) for low, high in zip(edges, edges[1:])
    ]

    step_size = section_size(substep)
    side = 1.0 - 2.0 * (lax.axis_index("ax") % 2).astype(jnp.float32)
    total_cells = checkpoint.shape[0] * count * checkpoint.shape[2]
    norm_factor = (patches / total_cells) ** 0.5
    gradient = (step_size * radial_diffusion[-1] * norm_factor) * binned[0]
    scal = jnp.stack([step_size, side])
    coef = jnp.stack([axial_speed, radial_diffusion, azimuth_diffusion], axis=1)
    half = 0.5 * side * step_size
    weight = jnp.stack(
        [step_size + half * axial_speed, jnp.broadcast_to(0.5 * half, axial_speed.shape)], axis=1
    )

    term = cot_term(scal, cot_far_rows, checkpoint, coef)
    term, cot_near, state_near = lax.optimization_barrier((term, cot_near, state_near))
    advanced, adjoint = local_parts(
        scal, checkpoint, state_near, cotangent, cot_near, term, wall, coef
    )
    bases = [advanced[:, low:high] for low, high in zip(edges[1:], edges[2:])]
    advanced, *bases = lax.optimization_barrier((advanced, *bases))
    advanced = add_rows(advanced, state_far_rows[0], weight, 0)
    for low, base, part in zip(edges[1:], bases, state_far_rows[1:]):
        advanced = put_rows(advanced, base, part, weight, low)
    return (advanced, adjoint, gradient)


def solution(mesh):
    placed = (
        P(("case", "ax"), None, None),
        P(("case", "ax"), None, None),
        P("case"),
        P(("case", "ax"), None),
        P("case"),
        P(),
        P(),
        P(),
    )
    return jax.shard_map(
        local,
        mesh=mesh,
        in_specs=placed,
        out_specs=(P(("case", "ax"), None, None), P(("case", "ax"), None, None), P("case")),
        check_vma=False,
    )
```

```python
import math

import jax
import jax.numpy as jnp
from jax import lax
from jax.experimental import pallas as pl
from jax.experimental.pallas import tpu as pltpu
from jax.sharding import PartitionSpec as P

time_step = 0.6
dissipation = 2.0

STATE_PARTS = 48
STATE_CUTS = (0, 33, 44, 48)
LOCAL_ROWS = 96
FAR_WEIGHT = 100000
ADD_ROWS = 88
SUB = 8


def section_size(substep):
    section_table = jnp.array([1.0 / 3.0, 15.0 / 16.0, 8.0 / 15.0], jnp.float32) * time_step
    selector = (jnp.arange(3, dtype=jnp.int32) == substep[0]).astype(jnp.float32)
    return jnp.sum(section_table * selector)


def on_pairs(count):
    return [(i, i ^ 1) for i in range(count)]


def off_pairs(count):
    return [(i, (i + 1) % count if i % 2 else (i - 1) % count) for i in range(count)]


def cell_sum(value, axis):
    count = lax.axis_size(axis)
    direct = [i for i in range(count) if i % 4 in (1, 2)]
    turning = [i for i in range(count) if i % 4 in (0, 3)]
    place = lax.axis_index(axis) % 4
    turns = (place == 0) | (place == 3)
    value = value + lax.ppermute(value, axis, [(i, i ^ 1) for i in range(count)])
    for n in range(2, count.bit_length() - 1):
        value = value + lax.ppermute(value, axis, [(i, i ^ (1 << n)) for i in direct])
    given = lax.ppermute(value, axis, [(i, i ^ 1) for i in direct])
    value = given + lax.ppermute(given, axis, [(i, i ^ 3) for i in turning])
    return jnp.where(turns, value, lax.ppermute(value, axis, [(i, i ^ 1) for i in turning]))


def wall_kernel(ids, amplitudes, edge, wall, bins):
    patches, cells = amplitudes.shape[1], ids.shape[1]
    patch = lax.broadcasted_iota(jnp.int32, (patches, cells), 0)
    hit = jnp.where(patch == ids[...], 1.0, 0.0).astype(jnp.float32)
    values = jnp.broadcast_to(amplitudes[...], (SUB, patches))
    wall[...] = lax.dot_general(
        values,
        hit,
        (((1,), (0,)), ((), ())),
        precision=lax.Precision.HIGHEST,
        preferred_element_type=jnp.float32,
    )[:1]
    bins[...] = lax.dot_general(
        edge[0],
        hit,
        (((1,), (1,)), ((), ())),
        precision=lax.Precision.HIGHEST,
        preferred_element_type=jnp.float32,
    )[SUB - 1 :]


def wall_and_bins(patch_ids, amplitudes, cotangent):
    rows, cells = cotangent.shape[1:]
    patches = amplitudes.shape[0]
    return pl.pallas_call(
        wall_kernel,
        grid=(1,),
        out_shape=(
            jax.ShapeDtypeStruct((1, cells), jnp.float32),
            jax.ShapeDtypeStruct((1, patches), jnp.float32),
        ),
        in_specs=[
            pl.BlockSpec((1, cells), lambda i: (0, 0)),
            pl.BlockSpec((1, patches), lambda i: (0, 0)),
            pl.BlockSpec((1, SUB, cells), lambda i: (0, rows // SUB - 1, 0)),
        ],
        out_specs=(
            pl.BlockSpec((1, cells), lambda i: (0, 0)),
            pl.BlockSpec((1, patches), lambda i: (0, 0)),
        ),
        compiler_params=pltpu.CompilerParams(vmem_limit_bytes=40 << 20),
    )(patch_ids, amplitudes[None], cotangent)


def local_kernel(scal, q, q_up, q_down, q_near, c, c_up, c_down, c_near, far, wall, coef, q_out, c_out):
    block, width = q.shape[1:]
    step, side = scal[0], scal[1]
    here, last = pl.program_id(0), pl.num_programs(0) - 1
    u, rd, ad = coef[:, 0:1], coef[:, 1:2], coef[:, 2:3]
    row = lax.broadcasted_iota(jnp.int32, (block, 1), 0)

    def around(x, up, down):
        above = jnp.where(row == 0, up, pltpu.roll(x, 1, 0))
        below = jnp.where(row == block - 1, down, pltpu.roll(x, block - 1, 0))
        return above, below

    def sides(x):
        return pltpu.roll(x, 1, 1) + pltpu.roll(x, width - 1, 1)

    x = q[0]
    first_row = pltpu.roll(x[:1], width // 2, 1)
    up = jnp.where(here == 0, first_row, q_up[0, SUB - 1 :])
    down = jnp.where(here == last, wall[...], q_down[0, :1])
    above, below = around(x, up, down)
    near = q_near[0]
    axial = near - (0.5 * side) * (near * (u + 0.5 * near)) - dissipation * x
    q_out[0] = x + step * (
        axial + rd * (above + below - 2.0 * x) + ad * (sides(x) - 2.0 * x)
    )

    y = c[0]
    weighted = rd * y
    before, after = coef_rows(coef)
    first_row = pltpu.roll(weighted[:1], width // 2, 1)
    up = jnp.where(here == 0, first_row, before * c_up[0, SUB - 1 :])
    down = jnp.where(here == last, 0.0, after * c_down[0, :1])
    above, below = around(weighted, up, down)
    slope = (0.5 * side) * (u + x)
    axial = c_near[0] * (1.0 + slope) - dissipation * y
    c_out[0] = y + far[0] + step * (
        axial + (above + below - 2.0 * weighted) + ad * (sides(y) - 2.0 * y)
    )


def coef_rows(coef):
    return coef[0:1, 3:4], coef[0:1, 4:5]


def local_parts(scal, q, q_near, c, c_near, far, wall, coef):
    rows, width = q.shape[1:]
    block = math.gcd(LOCAL_ROWS, rows)
    tiles, total = block // SUB, rows // SUB
    full = pl.BlockSpec((1, block, width), lambda i: (0, i, 0))
    up = pl.BlockSpec((1, SUB, width), lambda i: (0, jnp.maximum(i * tiles - 1, 0), 0))
    down = pl.BlockSpec((1, SUB, width), lambda i: (0, jnp.minimum((i + 1) * tiles, total - 1), 0))
    rd = coef[:, 1]
    before, after = jnp.roll(rd, 1), jnp.roll(rd, -block)
    coef = jnp.concatenate([coef, before[:, None], after[:, None]], axis=1)
    shape = jax.ShapeDtypeStruct(q.shape, q.dtype)
    return pl.pallas_call(
        local_kernel,
        grid=(rows // block,),
        out_shape=(shape, shape),
        in_specs=[pl.BlockSpec(memory_space=pltpu.SMEM)]
        + [full, up, down, full] * 2
        + [full]
        + [pl.BlockSpec((1, width), lambda i: (0, 0))]
        + [pl.BlockSpec((block, coef.shape[1]), lambda i: (i, 0))],
        out_specs=(full, full),
        compiler_params=pltpu.CompilerParams(vmem_limit_bytes=40 << 20),
        cost_estimate=pl.CostEstimate(
            flops=50 * rows * width, bytes_accessed=4 * rows * width * 7, transcendentals=0
        ),
    )(scal, q, q, q, q_near, c, c, c, c_near, far, wall, coef)


def cot_kernel(scal, far, state, coef, out):
    out[0] = scal[0] * far[0] * (1.0 - (0.5 * scal[1]) * (coef[:, 0:1] + state[0]))


def cot_term(scal, far, state, coef):
    rows, width = far.shape[1:]
    block = math.gcd(128, rows)
    full = pl.BlockSpec((1, block, width), lambda i: (0, i, 0))
    return pl.pallas_call(
        cot_kernel,
        grid=(rows // block,),
        out_shape=jax.ShapeDtypeStruct(far.shape, far.dtype),
        in_specs=[pl.BlockSpec(memory_space=pltpu.SMEM), full, full]
        + [pl.BlockSpec((block, coef.shape[1]), lambda i: (i, 0))],
        out_specs=full,
        compiler_params=pltpu.CompilerParams(vmem_limit_bytes=40 << 20),
        cost_estimate=pl.CostEstimate(
            flops=FAR_WEIGHT * rows * width, bytes_accessed=4 * rows * width * 3, transcendentals=0
        ),
    )(scal, far, state, coef)


def state_far(base, far, weight, out):
    x = far[0]
    out[0] = base[0] + x * (weight[:, 0:1] + weight[:, 1:2] * x)


def add_rows(base, part, weight, start):
    rows, width = part.shape[1:]
    whole = rows <= ADD_ROWS and start % rows == 0
    block = rows if whole else math.gcd(ADD_ROWS, rows, start)
    first = start // block
    full = pl.BlockSpec((1, block, width), lambda i: (0, first + i, 0))
    piece = pl.BlockSpec((1, block, width), lambda i: (0, i, 0))
    column = pl.BlockSpec((block, weight.shape[1]), lambda i: (first + i, 0))
    return pl.pallas_call(
        state_far,
        grid=(rows // block,),
        out_shape=jax.ShapeDtypeStruct(base.shape, base.dtype),
        in_specs=[full, piece, column],
        out_specs=full,
        input_output_aliases={0: 0},
        compiler_params=pltpu.CompilerParams(vmem_limit_bytes=40 << 20),
        cost_estimate=pl.CostEstimate(
            flops=10 * rows * width, bytes_accessed=4 * rows * width * 3, transcendentals=0
        ),
    )(base, part, weight)


def put_rows(out, base, part, weight, start):
    rows, width = part.shape[1:]

    def kernel(base, far, weight, before, out, fresh, sem):
        x = far[0]
        of_row = weight[pl.ds(start, rows), :]
        fresh[...] = base[0] + x * (of_row[:, 0:1] + of_row[:, 1:2] * x)
        store = pltpu.make_async_copy(fresh, out.at[0, pl.ds(start, rows)], sem)
        store.start()
        store.wait()

    anywhere = pl.BlockSpec(memory_space=pl.ANY)
    return pl.pallas_call(
        kernel,
        out_shape=jax.ShapeDtypeStruct(out.shape, out.dtype),
        in_specs=[pl.BlockSpec(memory_space=pltpu.VMEM)] * 3 + [anywhere],
        out_specs=anywhere,
        scratch_shapes=[pltpu.VMEM((rows, width), jnp.float32), pltpu.SemaphoreType.DMA],
        input_output_aliases={3: 0},
        compiler_params=pltpu.CompilerParams(vmem_limit_bytes=40 << 20),
        cost_estimate=pl.CostEstimate(
            flops=10 * rows * width, bytes_accessed=4 * rows * width * 3, transcendentals=0
        ),
    )(base, part, weight, out)


def local(
    checkpoint,
    cotangent,
    amplitudes,
    patch_ids,
    substep,
    axial_speed,
    radial_diffusion,
    azimuth_diffusion,
):
    count = lax.axis_size("ax")
    rows = checkpoint.shape[1]
    patches = amplitudes.shape[0]
    far = off_pairs(count)
    cot_far_rows = lax.ppermute(cotangent, "ax", far)

    wall, binned = wall_and_bins(patch_ids, amplitudes, cotangent)
    if count & (count - 1) or count < 4:
        binned = lax.psum(binned, "ax")
    else:
        binned = cell_sum(binned, "ax")

    late, cot_late, binned = lax.optimization_barrier((checkpoint, cotangent, binned))
    cot_near = lax.ppermute(cot_late, "ax", on_pairs(count))
    state_near = lax.ppermute(late, "ax", on_pairs(count))
    edges = [rows * n // STATE_PARTS for n in STATE_CUTS]
    state_far_rows = [
        lax.ppermute(late[:, low:high], "ax", far) for low, high in zip(edges, edges[1:])
    ]

    step_size = section_size(substep)
    side = 1.0 - 2.0 * (lax.axis_index("ax") % 2).astype(jnp.float32)
    total_cells = checkpoint.shape[0] * count * checkpoint.shape[2]
    norm_factor = (patches / total_cells) ** 0.5
    gradient = (step_size * radial_diffusion[-1] * norm_factor) * binned[0]
    scal = jnp.stack([step_size, side])
    coef = jnp.stack([axial_speed, radial_diffusion, azimuth_diffusion], axis=1)
    half = 0.5 * side * step_size
    weight = jnp.stack(
        [step_size + half * axial_speed, jnp.broadcast_to(0.5 * half, axial_speed.shape)], axis=1
    )

    term = cot_term(scal, cot_far_rows, checkpoint, coef)
    term, cot_near, state_near = lax.optimization_barrier((term, cot_near, state_near))
    advanced, adjoint = local_parts(
        scal, checkpoint, state_near, cotangent, cot_near, term, wall, coef
    )
    bases = [advanced[:, low:high] for low, high in zip(edges[1:], edges[2:])]
    advanced, *bases = lax.optimization_barrier((advanced, *bases))
    advanced = add_rows(advanced, state_far_rows[0], weight, 0)
    for low, base, part in zip(edges[1:], bases, state_far_rows[1:]):
        advanced = put_rows(advanced, base, part, weight, low)
    return (advanced, adjoint, gradient)


def solution(mesh):
    placed = (
        P(("case", "ax"), None, None),
        P(("case", "ax"), None, None),
        P("case"),
        P(("case", "ax"), None),
        P("case"),
        P(),
        P(),
        P(),
    )
    return jax.shard_map(
        local,
        mesh=mesh,
        in_specs=placed,
        out_specs=(P(("case", "ax"), None, None), P(("case", "ax"), None, None), P("case")),
        check_vma=False,
    )
```

```python
import math

import jax
import jax.numpy as jnp
from jax import lax
from jax.experimental import pallas as pl
from jax.experimental.pallas import tpu as pltpu
from jax.sharding import PartitionSpec as P

time_step = 0.6
dissipation = 2.0

STATE_PARTS = 16
STATE_CUTS = (0, 11, 15, 16)
LOCAL_ROWS = 64
ADD_ROWS = 88
SUB = 8


def section_size(substep):
    section_table = jnp.array([1.0 / 3.0, 15.0 / 16.0, 8.0 / 15.0], jnp.float32) * time_step
    selector = (jnp.arange(3, dtype=jnp.int32) == substep[0]).astype(jnp.float32)
    return jnp.sum(section_table * selector)


def on_pairs(count):
    return [(i, i ^ 1) for i in range(count)]


def off_pairs(count):
    return [(i, (i + 1) % count if i % 2 else (i - 1) % count) for i in range(count)]


def cell_sum(value, axis):
    count = lax.axis_size(axis)
    direct = [i for i in range(count) if i % 4 in (1, 2)]
    turning = [i for i in range(count) if i % 4 in (0, 3)]
    place = lax.axis_index(axis) % 4
    turns = (place == 0) | (place == 3)
    value = value + lax.ppermute(value, axis, [(i, i ^ 1) for i in range(count)])
    for n in range(2, count.bit_length() - 1):
        value = value + lax.ppermute(value, axis, [(i, i ^ (1 << n)) for i in direct])
    given = lax.ppermute(value, axis, [(i, i ^ 1) for i in direct])
    value = given + lax.ppermute(given, axis, [(i, i ^ 3) for i in turning])
    return jnp.where(turns, value, lax.ppermute(value, axis, [(i, i ^ 1) for i in turning]))


def wall_kernel(ids, amplitudes, edge, wall, bins):
    patches, cells = amplitudes.shape[1], ids.shape[1]
    patch = lax.broadcasted_iota(jnp.int32, (patches, cells), 0)
    hit = jnp.where(patch == ids[...], 1.0, 0.0).astype(jnp.float32)
    values = jnp.broadcast_to(amplitudes[...], (SUB, patches))
    wall[...] = lax.dot_general(
        values,
        hit,
        (((1,), (0,)), ((), ())),
        precision=lax.Precision.HIGHEST,
        preferred_element_type=jnp.float32,
    )[:1]
    bins[...] = lax.dot_general(
        edge[0],
        hit,
        (((1,), (1,)), ((), ())),
        precision=lax.Precision.HIGHEST,
        preferred_element_type=jnp.float32,
    )[SUB - 1 :]


def wall_and_bins(patch_ids, amplitudes, cotangent):
    rows, cells = cotangent.shape[1:]
    patches = amplitudes.shape[0]
    return pl.pallas_call(
        wall_kernel,
        grid=(1,),
        out_shape=(
            jax.ShapeDtypeStruct((1, cells), jnp.float32),
            jax.ShapeDtypeStruct((1, patches), jnp.float32),
        ),
        in_specs=[
            pl.BlockSpec((1, cells), lambda i: (0, 0)),
            pl.BlockSpec((1, patches), lambda i: (0, 0)),
            pl.BlockSpec((1, SUB, cells), lambda i: (0, rows // SUB - 1, 0)),
        ],
        out_specs=(
            pl.BlockSpec((1, cells), lambda i: (0, 0)),
            pl.BlockSpec((1, patches), lambda i: (0, 0)),
        ),
        compiler_params=pltpu.CompilerParams(vmem_limit_bytes=40 << 20),
    )(patch_ids, amplitudes[None], cotangent)


def local_kernel(scal, q, q_up, q_down, q_near, c, c_up, c_down, c_near, c_far, wall, coef, q_out, c_out):
    block, width = q.shape[1:]
    step, side = scal[0], scal[1]
    here, last = pl.program_id(0), pl.num_programs(0) - 1
    u, rd, ad = coef[:, 0:1], coef[:, 1:2], coef[:, 2:3]
    row = lax.broadcasted_iota(jnp.int32, (block, 1), 0)

    def around(x, up, down):
        above = jnp.where(row == 0, up, pltpu.roll(x, 1, 0))
        below = jnp.where(row == block - 1, down, pltpu.roll(x, block - 1, 0))
        return above, below

    def sides(x):
        return pltpu.roll(x, 1, 1) + pltpu.roll(x, width - 1, 1)

    x = q[0]
    first_row = pltpu.roll(x[:1], width // 2, 1)
    up = jnp.where(here == 0, first_row, q_up[0, SUB - 1 :])
    down = jnp.where(here == last, wall[...], q_down[0, :1])
    above, below = around(x, up, down)
    near = q_near[0]
    axial = near - (0.5 * side) * (near * (u + 0.5 * near)) - dissipation * x
    q_out[0] = x + step * (
        axial + rd * (above + below - 2.0 * x) + ad * (sides(x) - 2.0 * x)
    )

    y = c[0]
    weighted = rd * y
    before, after = coef_rows(coef)
    first_row = pltpu.roll(weighted[:1], width // 2, 1)
    up = jnp.where(here == 0, first_row, before * c_up[0, SUB - 1 :])
    down = jnp.where(here == last, 0.0, after * c_down[0, :1])
    above, below = around(weighted, up, down)
    slope = (0.5 * side) * (u + x)
    axial = c_near[0] * (1.0 + slope) + c_far[0] * (1.0 - slope) - dissipation * y
    c_out[0] = y + step * (
        axial + (above + below - 2.0 * weighted) + ad * (sides(y) - 2.0 * y)
    )


def coef_rows(coef):
    return coef[0:1, 3:4], coef[0:1, 4:5]


def local_parts(scal, q, q_near, c, c_near, c_far, wall, coef):
    rows, width = q.shape[1:]
    block = math.gcd(LOCAL_ROWS, rows)
    tiles, total = block // SUB, rows // SUB
    full = pl.BlockSpec((1, block, width), lambda i: (0, i, 0))
    up = pl.BlockSpec((1, SUB, width), lambda i: (0, jnp.maximum(i * tiles - 1, 0), 0))
    down = pl.BlockSpec((1, SUB, width), lambda i: (0, jnp.minimum((i + 1) * tiles, total - 1), 0))
    rd = coef[:, 1]
    before, after = jnp.roll(rd, 1), jnp.roll(rd, -block)
    coef = jnp.concatenate([coef, before[:, None], after[:, None]], axis=1)
    shape = jax.ShapeDtypeStruct(q.shape, q.dtype)
    return pl.pallas_call(
        local_kernel,
        grid=(rows // block,),
        out_shape=(shape, shape),
        in_specs=[pl.BlockSpec(memory_space=pltpu.SMEM)]
        + [full, up, down, full] * 2
        + [full]
        + [pl.BlockSpec((1, width), lambda i: (0, 0))]
        + [pl.BlockSpec((block, coef.shape[1]), lambda i: (i, 0))],
        out_specs=(full, full),
        compiler_params=pltpu.CompilerParams(vmem_limit_bytes=40 << 20),
        cost_estimate=pl.CostEstimate(
            flops=50 * rows * width, bytes_accessed=4 * rows * width * 7, transcendentals=0
        ),
    )(scal, q, q, q, q_near, c, c, c, c_near, c_far, wall, coef)


def state_far(base, far, weight, out):
    x = far[0]
    out[0] = base[0] + x * (weight[:, 0:1] + weight[:, 1:2] * x)


def add_rows(base, part, weight, start):
    rows, width = part.shape[1:]
    whole = rows <= ADD_ROWS and start % rows == 0
    block = rows if whole else math.gcd(ADD_ROWS, rows, start)
    first = start // block
    full = pl.BlockSpec((1, block, width), lambda i: (0, first + i, 0))
    piece = pl.BlockSpec((1, block, width), lambda i: (0, i, 0))
    column = pl.BlockSpec((block, weight.shape[1]), lambda i: (first + i, 0))
    return pl.pallas_call(
        state_far,
        grid=(rows // block,),
        out_shape=jax.ShapeDtypeStruct(base.shape, base.dtype),
        in_specs=[full, piece, column],
        out_specs=full,
        input_output_aliases={0: 0},
        compiler_params=pltpu.CompilerParams(vmem_limit_bytes=40 << 20),
        cost_estimate=pl.CostEstimate(
            flops=10 * rows * width, bytes_accessed=4 * rows * width * 3, transcendentals=0
        ),
    )(base, part, weight)


def put_rows(out, base, part, weight, start):
    rows, width = part.shape[1:]

    def kernel(base, far, weight, before, out, fresh, sem):
        x = far[0]
        of_row = weight[pl.ds(start, rows), :]
        fresh[...] = base[0] + x * (of_row[:, 0:1] + of_row[:, 1:2] * x)
        store = pltpu.make_async_copy(fresh, out.at[0, pl.ds(start, rows)], sem)
        store.start()
        store.wait()

    anywhere = pl.BlockSpec(memory_space=pl.ANY)
    return pl.pallas_call(
        kernel,
        out_shape=jax.ShapeDtypeStruct(out.shape, out.dtype),
        in_specs=[pl.BlockSpec(memory_space=pltpu.VMEM)] * 3 + [anywhere],
        out_specs=anywhere,
        scratch_shapes=[pltpu.VMEM((rows, width), jnp.float32), pltpu.SemaphoreType.DMA],
        input_output_aliases={3: 0},
        compiler_params=pltpu.CompilerParams(vmem_limit_bytes=40 << 20),
        cost_estimate=pl.CostEstimate(
            flops=10 * rows * width, bytes_accessed=4 * rows * width * 3, transcendentals=0
        ),
    )(base, part, weight, out)


def local(
    checkpoint,
    cotangent,
    amplitudes,
    patch_ids,
    substep,
    axial_speed,
    radial_diffusion,
    azimuth_diffusion,
):
    count = lax.axis_size("ax")
    rows = checkpoint.shape[1]
    patches = amplitudes.shape[0]
    near, far = on_pairs(count), off_pairs(count)
    cot_far_rows = lax.ppermute(cotangent, "ax", far)
    cot_near_rows = lax.ppermute(cotangent, "ax", near)
    state_near_rows = lax.ppermute(checkpoint, "ax", near)

    wall, binned = wall_and_bins(patch_ids, amplitudes, cotangent)
    if count & (count - 1) or count < 4:
        binned = lax.psum(binned, "ax")
    else:
        binned = cell_sum(binned, "ax")

    late, binned = lax.optimization_barrier((checkpoint, binned))
    edges = [rows * n // STATE_PARTS for n in STATE_CUTS]
    state_far_rows = [
        lax.ppermute(late[:, low:high], "ax", far) for low, high in zip(edges, edges[1:])
    ]

    step_size = section_size(substep)
    side = 1.0 - 2.0 * (lax.axis_index("ax") % 2).astype(jnp.float32)
    total_cells = checkpoint.shape[0] * count * checkpoint.shape[2]
    norm_factor = (patches / total_cells) ** 0.5
    gradient = (step_size * radial_diffusion[-1] * norm_factor) * binned[0]
    scal = jnp.stack([step_size, side])
    coef = jnp.stack([axial_speed, radial_diffusion, azimuth_diffusion], axis=1)
    half = 0.5 * side * step_size
    weight = jnp.stack(
        [step_size + half * axial_speed, jnp.broadcast_to(0.5 * half, axial_speed.shape)], axis=1
    )

    cot_far_rows, cot_near_rows, state_near_rows = lax.optimization_barrier(
        (cot_far_rows, cot_near_rows, state_near_rows)
    )
    advanced, adjoint = local_parts(
        scal, checkpoint, state_near_rows, cotangent, cot_near_rows, cot_far_rows, wall, coef
    )
    bases = [advanced[:, low:high] for low, high in zip(edges[1:], edges[2:])]
    advanced, *bases = lax.optimization_barrier((advanced, *bases))
    advanced = add_rows(advanced, state_far_rows[0], weight, 0)
    for low, base, part in zip(edges[1:], bases, state_far_rows[1:]):
        advanced = put_rows(advanced, base, part, weight, low)
    return (advanced, adjoint, gradient)


def solution(mesh):
    placed = (
        P(("case", "ax"), None, None),
        P(("case", "ax"), None, None),
        P("case"),
        P(("case", "ax"), None),
        P("case"),
        P(),
        P(),
        P(),
    )
    return jax.shard_map(
        local,
        mesh=mesh,
        in_specs=placed,
        out_specs=(P(("case", "ax"), None, None), P(("case", "ax"), None, None), P("case")),
        check_vma=False,
    )
```

```python
import math

import jax
import jax.numpy as jnp
from jax import lax
from jax.experimental import pallas as pl
from jax.experimental.pallas import tpu as pltpu
from jax.sharding import PartitionSpec as P

time_step = 0.6
dissipation = 2.0

STATE_PARTS = 12
STATE_CUTS = (0, 11, 12)
LOCAL_ROWS = 64
SUB = 8


def section_size(substep):
    section_table = jnp.array([1.0 / 3.0, 15.0 / 16.0, 8.0 / 15.0], jnp.float32) * time_step
    selector = (jnp.arange(3, dtype=jnp.int32) == substep[0]).astype(jnp.float32)
    return jnp.sum(section_table * selector)


def on_pairs(count):
    return [(i, i ^ 1) for i in range(count)]


def off_pairs(count):
    return [(i, (i + 1) % count if i % 2 else (i - 1) % count) for i in range(count)]


def cell_sum(value, axis):
    count = lax.axis_size(axis)
    direct = [i for i in range(count) if i % 4 in (1, 2)]
    turning = [i for i in range(count) if i % 4 in (0, 3)]
    place = lax.axis_index(axis) % 4
    turns = (place == 0) | (place == 3)
    value = value + lax.ppermute(value, axis, [(i, i ^ 1) for i in range(count)])
    for n in range(2, count.bit_length() - 1):
        value = value + lax.ppermute(value, axis, [(i, i ^ (1 << n)) for i in direct])
    given = lax.ppermute(value, axis, [(i, i ^ 1) for i in direct])
    value = given + lax.ppermute(given, axis, [(i, i ^ 3) for i in turning])
    return jnp.where(turns, value, lax.ppermute(value, axis, [(i, i ^ 1) for i in turning]))


def wall_kernel(ids, amplitudes, edge, wall, bins):
    patches, cells = amplitudes.shape[1], ids.shape[1]
    patch = lax.broadcasted_iota(jnp.int32, (patches, cells), 0)
    hit = jnp.where(patch == ids[...], 1.0, 0.0).astype(jnp.float32)
    values = jnp.broadcast_to(amplitudes[...], (SUB, patches))
    wall[...] = lax.dot_general(
        values,
        hit,
        (((1,), (0,)), ((), ())),
        precision=lax.Precision.HIGHEST,
        preferred_element_type=jnp.float32,
    )[:1]
    bins[...] = lax.dot_general(
        edge[0],
        hit,
        (((1,), (1,)), ((), ())),
        precision=lax.Precision.HIGHEST,
        preferred_element_type=jnp.float32,
    )[SUB - 1 :]


def wall_and_bins(patch_ids, amplitudes, cotangent):
    rows, cells = cotangent.shape[1:]
    patches = amplitudes.shape[0]
    return pl.pallas_call(
        wall_kernel,
        grid=(1,),
        out_shape=(
            jax.ShapeDtypeStruct((1, cells), jnp.float32),
            jax.ShapeDtypeStruct((1, patches), jnp.float32),
        ),
        in_specs=[
            pl.BlockSpec((1, cells), lambda i: (0, 0)),
            pl.BlockSpec((1, patches), lambda i: (0, 0)),
            pl.BlockSpec((1, SUB, cells), lambda i: (0, rows // SUB - 1, 0)),
        ],
        out_specs=(
            pl.BlockSpec((1, cells), lambda i: (0, 0)),
            pl.BlockSpec((1, patches), lambda i: (0, 0)),
        ),
        compiler_params=pltpu.CompilerParams(vmem_limit_bytes=40 << 20),
    )(patch_ids, amplitudes[None], cotangent)


def local_kernel(scal, q, q_up, q_down, q_near, c, c_up, c_down, c_near, c_far, wall, coef, q_out, c_out):
    block, width = q.shape[1:]
    step, side = scal[0], scal[1]
    here, last = pl.program_id(0), pl.num_programs(0) - 1
    u, rd, ad = coef[:, 0:1], coef[:, 1:2], coef[:, 2:3]
    row = lax.broadcasted_iota(jnp.int32, (block, 1), 0)

    def around(x, up, down):
        above = jnp.where(row == 0, up, pltpu.roll(x, 1, 0))
        below = jnp.where(row == block - 1, down, pltpu.roll(x, block - 1, 0))
        return above, below

    def sides(x):
        return pltpu.roll(x, 1, 1) + pltpu.roll(x, width - 1, 1)

    x = q[0]
    first_row = pltpu.roll(x[:1], width // 2, 1)
    up = jnp.where(here == 0, first_row, q_up[0, SUB - 1 :])
    down = jnp.where(here == last, wall[...], q_down[0, :1])
    above, below = around(x, up, down)
    near = q_near[0]
    axial = near - (0.5 * side) * (near * (u + 0.5 * near)) - dissipation * x
    q_out[0] = x + step * (
        axial + rd * (above + below - 2.0 * x) + ad * (sides(x) - 2.0 * x)
    )

    y = c[0]
    weighted = rd * y
    before, after = coef_rows(coef)
    first_row = pltpu.roll(weighted[:1], width // 2, 1)
    up = jnp.where(here == 0, first_row, before * c_up[0, SUB - 1 :])
    down = jnp.where(here == last, 0.0, after * c_down[0, :1])
    above, below = around(weighted, up, down)
    slope = (0.5 * side) * (u + x)
    axial = c_near[0] * (1.0 + slope) + c_far[0] * (1.0 - slope) - dissipation * y
    c_out[0] = y + step * (
        axial + (above + below - 2.0 * weighted) + ad * (sides(y) - 2.0 * y)
    )


def coef_rows(coef):
    return coef[0:1, 3:4], coef[0:1, 4:5]


def local_parts(scal, q, q_near, c, c_near, c_far, wall, coef):
    rows, width = q.shape[1:]
    block = math.gcd(LOCAL_ROWS, rows)
    tiles, total = block // SUB, rows // SUB
    full = pl.BlockSpec((1, block, width), lambda i: (0, i, 0))
    up = pl.BlockSpec((1, SUB, width), lambda i: (0, jnp.maximum(i * tiles - 1, 0), 0))
    down = pl.BlockSpec((1, SUB, width), lambda i: (0, jnp.minimum((i + 1) * tiles, total - 1), 0))
    rd = coef[:, 1]
    before, after = jnp.roll(rd, 1), jnp.roll(rd, -block)
    coef = jnp.concatenate([coef, before[:, None], after[:, None]], axis=1)
    shape = jax.ShapeDtypeStruct(q.shape, q.dtype)
    return pl.pallas_call(
        local_kernel,
        grid=(rows // block,),
        out_shape=(shape, shape),
        in_specs=[pl.BlockSpec(memory_space=pltpu.SMEM)]
        + [full, up, down, full] * 2
        + [full]
        + [pl.BlockSpec((1, width), lambda i: (0, 0))]
        + [pl.BlockSpec((block, coef.shape[1]), lambda i: (i, 0))],
        out_specs=(full, full),
        compiler_params=pltpu.CompilerParams(vmem_limit_bytes=40 << 20),
        cost_estimate=pl.CostEstimate(
            flops=50 * rows * width, bytes_accessed=4 * rows * width * 7, transcendentals=0
        ),
    )(scal, q, q, q, q_near, c, c, c, c_near, c_far, wall, coef)


def put_rows(out, base, part, weight, start):
    rows, width = part.shape[1:]

    def kernel(base, far, weight, before, out, fresh, sem):
        x = far[0]
        of_row = weight[pl.ds(start, rows), :]
        fresh[...] = base[0] + x * (of_row[:, 0:1] + of_row[:, 1:2] * x)
        store = pltpu.make_async_copy(fresh, out.at[0, pl.ds(start, rows)], sem)
        store.start()
        store.wait()

    anywhere = pl.BlockSpec(memory_space=pl.ANY)
    return pl.pallas_call(
        kernel,
        out_shape=jax.ShapeDtypeStruct(out.shape, out.dtype),
        in_specs=[pl.BlockSpec(memory_space=pltpu.VMEM)] * 3 + [anywhere],
        out_specs=anywhere,
        scratch_shapes=[pltpu.VMEM((rows, width), jnp.float32), pltpu.SemaphoreType.DMA],
        input_output_aliases={3: 0},
        compiler_params=pltpu.CompilerParams(vmem_limit_bytes=40 << 20),
        cost_estimate=pl.CostEstimate(
            flops=10 * rows * width, bytes_accessed=4 * rows * width * 3, transcendentals=0
        ),
    )(base, part, weight, out)


def local(
    checkpoint,
    cotangent,
    amplitudes,
    patch_ids,
    substep,
    axial_speed,
    radial_diffusion,
    azimuth_diffusion,
):
    count = lax.axis_size("ax")
    rows = checkpoint.shape[1]
    patches = amplitudes.shape[0]
    near, far = on_pairs(count), off_pairs(count)
    cot_far_rows = lax.ppermute(cotangent, "ax", far)
    cot_near_rows = lax.ppermute(cotangent, "ax", near)
    state_near_rows = lax.ppermute(checkpoint, "ax", near)

    wall, binned = wall_and_bins(patch_ids, amplitudes, cotangent)
    if count & (count - 1) or count < 4:
        binned = lax.psum(binned, "ax")
    else:
        binned = cell_sum(binned, "ax")

    late, binned = lax.optimization_barrier((checkpoint, binned))
    edges = [rows * n // STATE_PARTS for n in STATE_CUTS]
    state_far_rows = [
        lax.ppermute(late[:, low:high], "ax", far) for low, high in zip(edges, edges[1:])
    ]

    step_size = section_size(substep)
    side = 1.0 - 2.0 * (lax.axis_index("ax") % 2).astype(jnp.float32)
    total_cells = checkpoint.shape[0] * count * checkpoint.shape[2]
    norm_factor = (patches / total_cells) ** 0.5
    gradient = (step_size * radial_diffusion[-1] * norm_factor) * binned[0]
    scal = jnp.stack([step_size, side])
    coef = jnp.stack([axial_speed, radial_diffusion, azimuth_diffusion], axis=1)
    half = 0.5 * side * step_size
    weight = jnp.stack(
        [step_size + half * axial_speed, jnp.broadcast_to(0.5 * half, axial_speed.shape)], axis=1
    )

    cot_far_rows, cot_near_rows, state_near_rows = lax.optimization_barrier(
        (cot_far_rows, cot_near_rows, state_near_rows)
    )
    advanced, adjoint = local_parts(
        scal, checkpoint, state_near_rows, cotangent, cot_near_rows, cot_far_rows, wall, coef
    )
    bases = [advanced[:, low:high] for low, high in zip(edges, edges[1:])]
    advanced, *bases = lax.optimization_barrier((advanced, *bases))
    for low, base, part in zip(edges, bases, state_far_rows):
        advanced = put_rows(advanced, base, part, weight, low)
    return (advanced, adjoint, gradient)


def solution(mesh):
    placed = (
        P(("case", "ax"), None, None),
        P(("case", "ax"), None, None),
        P("case"),
        P(("case", "ax"), None),
        P("case"),
        P(),
        P(),
        P(),
    )
    return jax.shard_map(
        local,
        mesh=mesh,
        in_specs=placed,
        out_specs=(P(("case", "ax"), None, None), P(("case", "ax"), None, None), P("case")),
        check_vma=False,
    )
```

```python
import math

import jax
import jax.numpy as jnp
from jax import lax
from jax.experimental import pallas as pl
from jax.experimental.pallas import tpu as pltpu
from jax.sharding import PartitionSpec as P

time_step = 0.6
dissipation = 2.0

STATE_PARTS = 48
STATE_CUTS = (0, 33, 44, 48)
LOCAL_ROWS = 64
ADD_ROWS = 88
SUB = 8


def section_size(substep):
    section_table = jnp.array([1.0 / 3.0, 15.0 / 16.0, 8.0 / 15.0], jnp.float32) * time_step
    selector = (jnp.arange(3, dtype=jnp.int32) == substep[0]).astype(jnp.float32)
    return jnp.sum(section_table * selector)


def on_pairs(count):
    return [(i, i ^ 1) for i in range(count)]


def off_pairs(count):
    return [(i, (i + 1) % count if i % 2 else (i - 1) % count) for i in range(count)]


def cell_sum(value, axis):
    count = lax.axis_size(axis)
    direct = [i for i in range(count) if i % 4 in (1, 2)]
    turning = [i for i in range(count) if i % 4 in (0, 3)]
    place = lax.axis_index(axis) % 4
    turns = (place == 0) | (place == 3)
    value = value + lax.ppermute(value, axis, [(i, i ^ 1) for i in range(count)])
    for n in range(2, count.bit_length() - 1):
        value = value + lax.ppermute(value, axis, [(i, i ^ (1 << n)) for i in direct])
    given = lax.ppermute(value, axis, [(i, i ^ 1) for i in direct])
    value = given + lax.ppermute(given, axis, [(i, i ^ 3) for i in turning])
    return jnp.where(turns, value, lax.ppermute(value, axis, [(i, i ^ 1) for i in turning]))


def wall_kernel(ids, amplitudes, edge, wall, bins):
    patches, cells = amplitudes.shape[1], ids.shape[1]
    patch = lax.broadcasted_iota(jnp.int32, (patches, cells), 0)
    hit = jnp.where(patch == ids[...], 1.0, 0.0).astype(jnp.float32)
    values = jnp.broadcast_to(amplitudes[...], (SUB, patches))
    wall[...] = lax.dot_general(
        values,
        hit,
        (((1,), (0,)), ((), ())),
        precision=lax.Precision.HIGHEST,
        preferred_element_type=jnp.float32,
    )[:1]
    bins[...] = lax.dot_general(
        edge[0],
        hit,
        (((1,), (1,)), ((), ())),
        precision=lax.Precision.HIGHEST,
        preferred_element_type=jnp.float32,
    )[SUB - 1 :]


def wall_and_bins(patch_ids, amplitudes, cotangent):
    rows, cells = cotangent.shape[1:]
    patches = amplitudes.shape[0]
    return pl.pallas_call(
        wall_kernel,
        grid=(1,),
        out_shape=(
            jax.ShapeDtypeStruct((1, cells), jnp.float32),
            jax.ShapeDtypeStruct((1, patches), jnp.float32),
        ),
        in_specs=[
            pl.BlockSpec((1, cells), lambda i: (0, 0)),
            pl.BlockSpec((1, patches), lambda i: (0, 0)),
            pl.BlockSpec((1, SUB, cells), lambda i: (0, rows // SUB - 1, 0)),
        ],
        out_specs=(
            pl.BlockSpec((1, cells), lambda i: (0, 0)),
            pl.BlockSpec((1, patches), lambda i: (0, 0)),
        ),
        compiler_params=pltpu.CompilerParams(vmem_limit_bytes=40 << 20),
    )(patch_ids, amplitudes[None], cotangent)


def local_kernel(scal, q, q_up, q_down, q_near, c, c_up, c_down, c_near, c_far, wall, coef, q_out, c_out):
    block, width = q.shape[1:]
    step, side = scal[0], scal[1]
    here, last = pl.program_id(0), pl.num_programs(0) - 1
    u, rd, ad = coef[:, 0:1], coef[:, 1:2], coef[:, 2:3]
    row = lax.broadcasted_iota(jnp.int32, (block, 1), 0)

    def around(x, up, down):
        above = jnp.where(row == 0, up, pltpu.roll(x, 1, 0))
        below = jnp.where(row == block - 1, down, pltpu.roll(x, block - 1, 0))
        return above, below

    def sides(x):
        return pltpu.roll(x, 1, 1) + pltpu.roll(x, width - 1, 1)

    x = q[0]
    first_row = pltpu.roll(x[:1], width // 2, 1)
    up = jnp.where(here == 0, first_row, q_up[0, SUB - 1 :])
    down = jnp.where(here == last, wall[...], q_down[0, :1])
    above, below = around(x, up, down)
    near = q_near[0]
    axial = near - (0.5 * side) * (near * (u + 0.5 * near)) - dissipation * x
    q_out[0] = x + step * (
        axial + rd * (above + below - 2.0 * x) + ad * (sides(x) - 2.0 * x)
    )

    y = c[0]
    weighted = rd * y
    before, after = coef_rows(coef)
    first_row = pltpu.roll(weighted[:1], width // 2, 1)
    up = jnp.where(here == 0, first_row, before * c_up[0, SUB - 1 :])
    down = jnp.where(here == last, 0.0, after * c_down[0, :1])
    above, below = around(weighted, up, down)
    slope = (0.5 * side) * (u + x)
    axial = c_near[0] * (1.0 + slope) + c_far[0] * (1.0 - slope) - dissipation * y
    c_out[0] = y + step * (
        axial + (above + below - 2.0 * weighted) + ad * (sides(y) - 2.0 * y)
    )


def coef_rows(coef):
    return coef[0:1, 3:4], coef[0:1, 4:5]


def local_parts(scal, q, q_near, c, c_near, c_far, wall, coef):
    rows, width = q.shape[1:]
    block = math.gcd(LOCAL_ROWS, rows)
    tiles, total = block // SUB, rows // SUB
    full = pl.BlockSpec((1, block, width), lambda i: (0, i, 0))
    up = pl.BlockSpec((1, SUB, width), lambda i: (0, jnp.maximum(i * tiles - 1, 0), 0))
    down = pl.BlockSpec((1, SUB, width), lambda i: (0, jnp.minimum((i + 1) * tiles, total - 1), 0))
    rd = coef[:, 1]
    before, after = jnp.roll(rd, 1), jnp.roll(rd, -block)
    coef = jnp.concatenate([coef, before[:, None], after[:, None]], axis=1)
    shape = jax.ShapeDtypeStruct(q.shape, q.dtype)
    return pl.pallas_call(
        local_kernel,
        grid=(rows // block,),
        out_shape=(shape, shape),
        in_specs=[pl.BlockSpec(memory_space=pltpu.SMEM)]
        + [full, up, down, full] * 2
        + [full]
        + [pl.BlockSpec((1, width), lambda i: (0, 0))]
        + [pl.BlockSpec((block, coef.shape[1]), lambda i: (i, 0))],
        out_specs=(full, full),
        compiler_params=pltpu.CompilerParams(vmem_limit_bytes=40 << 20),
        cost_estimate=pl.CostEstimate(
            flops=50 * rows * width, bytes_accessed=4 * rows * width * 7, transcendentals=0
        ),
    )(scal, q, q, q, q_near, c, c, c, c_near, c_far, wall, coef)


def state_far(base, far, weight, out):
    x = far[0]
    out[0] = base[0] + x * (weight[:, 0:1] + weight[:, 1:2] * x)


def add_rows(base, part, weight, start):
    rows, width = part.shape[1:]
    whole = rows <= ADD_ROWS and start % rows == 0
    block = rows if whole else math.gcd(ADD_ROWS, rows, start)
    first = start // block
    full = pl.BlockSpec((1, block, width), lambda i: (0, first + i, 0))
    piece = pl.BlockSpec((1, block, width), lambda i: (0, i, 0))
    column = pl.BlockSpec((block, weight.shape[1]), lambda i: (first + i, 0))
    return pl.pallas_call(
        state_far,
        grid=(rows // block,),
        out_shape=jax.ShapeDtypeStruct(base.shape, base.dtype),
        in_specs=[full, piece, column],
        out_specs=full,
        input_output_aliases={0: 0},
        compiler_params=pltpu.CompilerParams(vmem_limit_bytes=40 << 20),
        cost_estimate=pl.CostEstimate(
            flops=10 * rows * width, bytes_accessed=4 * rows * width * 3, transcendentals=0
        ),
    )(base, part, weight)


def put_rows(out, base, part, weight, start):
    rows, width = part.shape[1:]

    def kernel(base, far, weight, before, out, fresh, sems):
        stores = []
        for n in range(rows // SUB):
            here = pl.ds(n * SUB, SUB)
            there = pl.ds(start + n * SUB, SUB)
            x = far[0, here]
            of_row = weight[there, :]
            fresh[here] = base[0, here] + x * (of_row[:, 0:1] + of_row[:, 1:2] * x)
            store = pltpu.make_async_copy(fresh.at[here], out.at[0, there], sems.at[n])
            store.start()
            stores.append(store)
        for store in stores:
            store.wait()

    anywhere = pl.BlockSpec(memory_space=pl.ANY)
    return pl.pallas_call(
        kernel,
        out_shape=jax.ShapeDtypeStruct(out.shape, out.dtype),
        in_specs=[pl.BlockSpec(memory_space=pltpu.VMEM)] * 3 + [anywhere],
        out_specs=anywhere,
        scratch_shapes=[
            pltpu.VMEM((rows, width), jnp.float32),
            pltpu.SemaphoreType.DMA((rows // SUB,)),
        ],
        input_output_aliases={3: 0},
        compiler_params=pltpu.CompilerParams(vmem_limit_bytes=40 << 20),
        cost_estimate=pl.CostEstimate(
            flops=10 * rows * width, bytes_accessed=4 * rows * width * 3, transcendentals=0
        ),
    )(base, part, weight, out)


def local(
    checkpoint,
    cotangent,
    amplitudes,
    patch_ids,
    substep,
    axial_speed,
    radial_diffusion,
    azimuth_diffusion,
):
    count = lax.axis_size("ax")
    rows = checkpoint.shape[1]
    patches = amplitudes.shape[0]
    near, far = on_pairs(count), off_pairs(count)
    cot_far_rows = lax.ppermute(cotangent, "ax", far)
    cot_near_rows = lax.ppermute(cotangent, "ax", near)
    state_near_rows = lax.ppermute(checkpoint, "ax", near)

    wall, binned = wall_and_bins(patch_ids, amplitudes, cotangent)
    if count & (count - 1) or count < 4:
        binned = lax.psum(binned, "ax")
    else:
        binned = cell_sum(binned, "ax")

    late, binned = lax.optimization_barrier((checkpoint, binned))
    edges = [rows * n // STATE_PARTS for n in STATE_CUTS]
    state_far_rows = [
        lax.ppermute(late[:, low:high], "ax", far) for low, high in zip(edges, edges[1:])
    ]

    step_size = section_size(substep)
    side = 1.0 - 2.0 * (lax.axis_index("ax") % 2).astype(jnp.float32)
    total_cells = checkpoint.shape[0] * count * checkpoint.shape[2]
    norm_factor = (patches / total_cells) ** 0.5
    gradient = (step_size * radial_diffusion[-1] * norm_factor) * binned[0]
    scal = jnp.stack([step_size, side])
    coef = jnp.stack([axial_speed, radial_diffusion, azimuth_diffusion], axis=1)
    half = 0.5 * side * step_size
    weight = jnp.stack(
        [step_size + half * axial_speed, jnp.broadcast_to(0.5 * half, axial_speed.shape)], axis=1
    )

    cot_far_rows, cot_near_rows, state_near_rows = lax.optimization_barrier(
        (cot_far_rows, cot_near_rows, state_near_rows)
    )
    advanced, adjoint = local_parts(
        scal, checkpoint, state_near_rows, cotangent, cot_near_rows, cot_far_rows, wall, coef
    )
    bases = [advanced[:, low:high] for low, high in zip(edges[1:], edges[2:])]
    advanced, *bases = lax.optimization_barrier((advanced, *bases))
    advanced = add_rows(advanced, state_far_rows[0], weight, 0)
    for low, base, part in zip(edges[1:], bases, state_far_rows[1:]):
        advanced = put_rows(advanced, base, part, weight, low)
    return (advanced, adjoint, gradient)


def solution(mesh):
    placed = (
        P(("case", "ax"), None, None),
        P(("case", "ax"), None, None),
        P("case"),
        P(("case", "ax"), None),
        P("case"),
        P(),
        P(),
        P(),
    )
    return jax.shard_map(
        local,
        mesh=mesh,
        in_specs=placed,
        out_specs=(P(("case", "ax"), None, None), P(("case", "ax"), None, None), P("case")),
        check_vma=False,
    )
```

```python
import math

import jax
import jax.numpy as jnp
from jax import lax
from jax.experimental import pallas as pl
from jax.experimental.pallas import tpu as pltpu
from jax.sharding import PartitionSpec as P

time_step = 0.6
dissipation = 2.0

STATE_PARTS = 48
STATE_CUTS = (0, 33, 44, 48)
LOCAL_ROWS = 64
ADD_ROWS = 88
SUB = 8


def section_size(substep):
    section_table = jnp.array([1.0 / 3.0, 15.0 / 16.0, 8.0 / 15.0], jnp.float32) * time_step
    selector = (jnp.arange(3, dtype=jnp.int32) == substep[0]).astype(jnp.float32)
    return jnp.sum(section_table * selector)


def on_pairs(count):
    return [(i, i ^ 1) for i in range(count)]


def off_pairs(count):
    return [(i, (i + 1) % count if i % 2 else (i - 1) % count) for i in range(count)]


def cell_sum(value, axis):
    count = lax.axis_size(axis)
    direct = [i for i in range(count) if i % 4 in (1, 2)]
    turning = [i for i in range(count) if i % 4 in (0, 3)]
    place = lax.axis_index(axis) % 4
    turns = (place == 0) | (place == 3)
    value = value + lax.ppermute(value, axis, [(i, i ^ 1) for i in range(count)])
    for n in range(2, count.bit_length() - 1):
        value = value + lax.ppermute(value, axis, [(i, i ^ (1 << n)) for i in direct])
    given = lax.ppermute(value, axis, [(i, i ^ 1) for i in direct])
    value = given + lax.ppermute(given, axis, [(i, i ^ 3) for i in turning])
    return jnp.where(turns, value, lax.ppermute(value, axis, [(i, i ^ 1) for i in turning]))


def wall_kernel(ids, amplitudes, edge, wall, bins):
    patches, cells = amplitudes.shape[1], ids.shape[1]
    patch = lax.broadcasted_iota(jnp.int32, (patches, cells), 0)
    hit = jnp.where(patch == ids[...], 1.0, 0.0).astype(jnp.float32)
    values = jnp.broadcast_to(amplitudes[...], (SUB, patches))
    wall[...] = lax.dot_general(
        values,
        hit,
        (((1,), (0,)), ((), ())),
        precision=lax.Precision.HIGHEST,
        preferred_element_type=jnp.float32,
    )[:1]
    bins[...] = lax.dot_general(
        edge[0],
        hit,
        (((1,), (1,)), ((), ())),
        precision=lax.Precision.HIGHEST,
        preferred_element_type=jnp.float32,
    )[SUB - 1 :]


def wall_and_bins(patch_ids, amplitudes, cotangent):
    rows, cells = cotangent.shape[1:]
    patches = amplitudes.shape[0]
    return pl.pallas_call(
        wall_kernel,
        grid=(1,),
        out_shape=(
            jax.ShapeDtypeStruct((1, cells), jnp.float32),
            jax.ShapeDtypeStruct((1, patches), jnp.float32),
        ),
        in_specs=[
            pl.BlockSpec((1, cells), lambda i: (0, 0)),
            pl.BlockSpec((1, patches), lambda i: (0, 0)),
            pl.BlockSpec((1, SUB, cells), lambda i: (0, rows // SUB - 1, 0)),
        ],
        out_specs=(
            pl.BlockSpec((1, cells), lambda i: (0, 0)),
            pl.BlockSpec((1, patches), lambda i: (0, 0)),
        ),
        compiler_params=pltpu.CompilerParams(vmem_limit_bytes=40 << 20),
    )(patch_ids, amplitudes[None], cotangent)


def local_kernel(scal, q, q_up, q_down, q_near, c, c_up, c_down, c_near, c_far, wall, coef, q_out, c_out):
    block, width = q.shape[1:]
    step, side = scal[0], scal[1]
    here, last = pl.program_id(0), pl.num_programs(0) - 1
    u, rd, ad = coef[:, 0:1], coef[:, 1:2], coef[:, 2:3]
    row = lax.broadcasted_iota(jnp.int32, (block, 1), 0)

    def around(x, up, down):
        above = jnp.where(row == 0, up, pltpu.roll(x, 1, 0))
        below = jnp.where(row == block - 1, down, pltpu.roll(x, block - 1, 0))
        return above, below

    def sides(x):
        return pltpu.roll(x, 1, 1) + pltpu.roll(x, width - 1, 1)

    x = q[0]
    first_row = pltpu.roll(x[:1], width // 2, 1)
    up = jnp.where(here == 0, first_row, q_up[0, SUB - 1 :])
    down = jnp.where(here == last, wall[...], q_down[0, :1])
    above, below = around(x, up, down)
    near = q_near[0]
    axial = near - (0.5 * side) * (near * (u + 0.5 * near)) - dissipation * x
    q_out[0] = x + step * (
        axial + rd * (above + below - 2.0 * x) + ad * (sides(x) - 2.0 * x)
    )

    y = c[0]
    weighted = rd * y
    before, after = coef_rows(coef)
    first_row = pltpu.roll(weighted[:1], width // 2, 1)
    up = jnp.where(here == 0, first_row, before * c_up[0, SUB - 1 :])
    down = jnp.where(here == last, 0.0, after * c_down[0, :1])
    above, below = around(weighted, up, down)
    slope = (0.5 * side) * (u + x)
    axial = c_near[0] * (1.0 + slope) + c_far[0] * (1.0 - slope) - dissipation * y
    c_out[0] = y + step * (
        axial + (above + below - 2.0 * weighted) + ad * (sides(y) - 2.0 * y)
    )


def coef_rows(coef):
    return coef[0:1, 3:4], coef[0:1, 4:5]


def local_parts(scal, q, q_near, c, c_near, c_far, wall, coef):
    rows, width = q.shape[1:]
    block = math.gcd(LOCAL_ROWS, rows)
    tiles, total = block // SUB, rows // SUB
    full = pl.BlockSpec((1, block, width), lambda i: (0, i, 0))
    up = pl.BlockSpec((1, SUB, width), lambda i: (0, jnp.maximum(i * tiles - 1, 0), 0))
    down = pl.BlockSpec((1, SUB, width), lambda i: (0, jnp.minimum((i + 1) * tiles, total - 1), 0))
    rd = coef[:, 1]
    before, after = jnp.roll(rd, 1), jnp.roll(rd, -block)
    coef = jnp.concatenate([coef, before[:, None], after[:, None]], axis=1)
    shape = jax.ShapeDtypeStruct(q.shape, q.dtype)
    return pl.pallas_call(
        local_kernel,
        grid=(rows // block,),
        out_shape=(shape, shape),
        in_specs=[pl.BlockSpec(memory_space=pltpu.SMEM)]
        + [full, up, down, full] * 2
        + [full]
        + [pl.BlockSpec((1, width), lambda i: (0, 0))]
        + [pl.BlockSpec((block, coef.shape[1]), lambda i: (i, 0))],
        out_specs=(full, full),
        compiler_params=pltpu.CompilerParams(vmem_limit_bytes=40 << 20),
        cost_estimate=pl.CostEstimate(
            flops=50 * rows * width, bytes_accessed=4 * rows * width * 7, transcendentals=0
        ),
    )(scal, q, q, q, q_near, c, c, c, c_near, c_far, wall, coef)


def state_far(base, far, weight, out):
    x = far[0]
    out[0] = base[0] + x * (weight[:, 0:1] + weight[:, 1:2] * x)


def add_rows(base, part, weight, start):
    rows, width = part.shape[1:]
    whole = rows <= ADD_ROWS and start % rows == 0
    block = rows if whole else math.gcd(ADD_ROWS, rows, start)
    first = start // block
    full = pl.BlockSpec((1, block, width), lambda i: (0, first + i, 0))
    piece = pl.BlockSpec((1, block, width), lambda i: (0, i, 0))
    column = pl.BlockSpec((block, weight.shape[1]), lambda i: (first + i, 0))
    return pl.pallas_call(
        state_far,
        grid=(rows // block,),
        out_shape=jax.ShapeDtypeStruct(base.shape, base.dtype),
        in_specs=[full, piece, column],
        out_specs=full,
        input_output_aliases={0: 0},
        compiler_params=pltpu.CompilerParams(vmem_limit_bytes=40 << 20),
        cost_estimate=pl.CostEstimate(
            flops=10 * rows * width, bytes_accessed=4 * rows * width * 3, transcendentals=0
        ),
    )(base, part, weight)


def put_rows(out, base, part, weight, start):
    rows, width = part.shape[1:]

    def kernel(base, far, weight, before, out, fresh, sem):
        x = far[0]
        of_row = weight[pl.ds(start, rows), :]
        fresh[...] = base[0] + x * (of_row[:, 0:1] + of_row[:, 1:2] * x)
        store = pltpu.make_async_copy(fresh, out.at[0, pl.ds(start, rows)], sem)
        store.start()
        store.wait()

    anywhere = pl.BlockSpec(memory_space=pl.ANY)
    return pl.pallas_call(
        kernel,
        out_shape=jax.ShapeDtypeStruct(out.shape, out.dtype),
        in_specs=[pl.BlockSpec(memory_space=pltpu.VMEM)] * 3 + [anywhere],
        out_specs=anywhere,
        scratch_shapes=[pltpu.VMEM((rows, width), jnp.float32), pltpu.SemaphoreType.DMA],
        input_output_aliases={3: 0},
        compiler_params=pltpu.CompilerParams(vmem_limit_bytes=40 << 20),
        cost_estimate=pl.CostEstimate(
            flops=10 * rows * width, bytes_accessed=4 * rows * width * 3, transcendentals=0
        ),
    )(base, part, weight, out)


def local(
    checkpoint,
    cotangent,
    amplitudes,
    patch_ids,
    substep,
    axial_speed,
    radial_diffusion,
    azimuth_diffusion,
):
    count = lax.axis_size("ax")
    rows = checkpoint.shape[1]
    patches = amplitudes.shape[0]
    near, far = on_pairs(count), off_pairs(count)
    cot_far_rows = lax.ppermute(cotangent, "ax", far)
    cot_near_rows = lax.ppermute(cotangent, "ax", near)
    state_near_rows = lax.ppermute(checkpoint, "ax", near)

    wall, binned = wall_and_bins(patch_ids, amplitudes, cotangent)
    if count & (count - 1) or count < 4:
        binned = lax.psum(binned, "ax")
    else:
        binned = cell_sum(binned, "ax")

    late, cot_near_rows = lax.optimization_barrier((checkpoint, cot_near_rows))
    edges = [rows * n // STATE_PARTS for n in STATE_CUTS]
    state_far_rows = [
        lax.ppermute(late[:, low:high], "ax", far) for low, high in zip(edges, edges[1:])
    ]

    step_size = section_size(substep)
    side = 1.0 - 2.0 * (lax.axis_index("ax") % 2).astype(jnp.float32)
    total_cells = checkpoint.shape[0] * count * checkpoint.shape[2]
    norm_factor = (patches / total_cells) ** 0.5
    gradient = (step_size * radial_diffusion[-1] * norm_factor) * binned[0]
    scal = jnp.stack([step_size, side])
    coef = jnp.stack([axial_speed, radial_diffusion, azimuth_diffusion], axis=1)
    half = 0.5 * side * step_size
    weight = jnp.stack(
        [step_size + half * axial_speed, jnp.broadcast_to(0.5 * half, axial_speed.shape)], axis=1
    )

    cot_far_rows, cot_near_rows, state_near_rows = lax.optimization_barrier(
        (cot_far_rows, cot_near_rows, state_near_rows)
    )
    advanced, adjoint = local_parts(
        scal, checkpoint, state_near_rows, cotangent, cot_near_rows, cot_far_rows, wall, coef
    )
    bases = [advanced[:, low:high] for low, high in zip(edges[1:], edges[2:])]
    advanced, *bases = lax.optimization_barrier((advanced, *bases))
    advanced = add_rows(advanced, state_far_rows[0], weight, 0)
    for low, base, part in zip(edges[1:], bases, state_far_rows[1:]):
        advanced = put_rows(advanced, base, part, weight, low)
    return (advanced, adjoint, gradient)


def solution(mesh):
    placed = (
        P(("case", "ax"), None, None),
        P(("case", "ax"), None, None),
        P("case"),
        P(("case", "ax"), None),
        P("case"),
        P(),
        P(),
        P(),
    )
    return jax.shard_map(
        local,
        mesh=mesh,
        in_specs=placed,
        out_specs=(P(("case", "ax"), None, None), P(("case", "ax"), None, None), P("case")),
        check_vma=False,
    )
```

```python
import math

import jax
import jax.numpy as jnp
from jax import lax
from jax.experimental import pallas as pl
from jax.experimental.pallas import tpu as pltpu
from jax.sharding import PartitionSpec as P

time_step = 0.6
dissipation = 2.0

STATE_PARTS = 48
STATE_CUTS = (0, 33, 44, 48)
LOCAL_ROWS = 64
ADD_ROWS = 88
SUB = 8


def section_size(substep):
    section_table = jnp.array([1.0 / 3.0, 15.0 / 16.0, 8.0 / 15.0], jnp.float32) * time_step
    selector = (jnp.arange(3, dtype=jnp.int32) == substep[0]).astype(jnp.float32)
    return jnp.sum(section_table * selector)


def on_pairs(count):
    return [(i, i ^ 1) for i in range(count)]


def off_pairs(count):
    return [(i, (i + 1) % count if i % 2 else (i - 1) % count) for i in range(count)]


def cell_sum(value, axis):
    count = lax.axis_size(axis)
    direct = [i for i in range(count) if i % 4 in (1, 2)]
    turning = [i for i in range(count) if i % 4 in (0, 3)]
    place = lax.axis_index(axis) % 4
    turns = (place == 0) | (place == 3)
    value = value + lax.ppermute(value, axis, [(i, i ^ 1) for i in range(count)])
    for n in range(2, count.bit_length() - 1):
        value = value + lax.ppermute(value, axis, [(i, i ^ (1 << n)) for i in direct])
    given = lax.ppermute(value, axis, [(i, i ^ 1) for i in direct])
    value = given + lax.ppermute(given, axis, [(i, i ^ 3) for i in turning])
    return jnp.where(turns, value, lax.ppermute(value, axis, [(i, i ^ 1) for i in turning]))


def wall_kernel(ids, amplitudes, edge, wall, bins):
    patches, cells = amplitudes.shape[1], ids.shape[1]
    patch = lax.broadcasted_iota(jnp.int32, (patches, cells), 0)
    hit = jnp.where(patch == ids[...], 1.0, 0.0).astype(jnp.float32)
    values = jnp.broadcast_to(amplitudes[...], (SUB, patches))
    wall[...] = lax.dot_general(
        values,
        hit,
        (((1,), (0,)), ((), ())),
        precision=lax.Precision.HIGHEST,
        preferred_element_type=jnp.float32,
    )[:1]
    bins[...] = lax.dot_general(
        edge[0],
        hit,
        (((1,), (1,)), ((), ())),
        precision=lax.Precision.HIGHEST,
        preferred_element_type=jnp.float32,
    )[SUB - 1 :]


def wall_and_bins(patch_ids, amplitudes, cotangent):
    rows, cells = cotangent.shape[1:]
    patches = amplitudes.shape[0]
    return pl.pallas_call(
        wall_kernel,
        grid=(1,),
        out_shape=(
            jax.ShapeDtypeStruct((1, cells), jnp.float32),
            jax.ShapeDtypeStruct((1, patches), jnp.float32),
        ),
        in_specs=[
            pl.BlockSpec((1, cells), lambda i: (0, 0)),
            pl.BlockSpec((1, patches), lambda i: (0, 0)),
            pl.BlockSpec((1, SUB, cells), lambda i: (0, rows // SUB - 1, 0)),
        ],
        out_specs=(
            pl.BlockSpec((1, cells), lambda i: (0, 0)),
            pl.BlockSpec((1, patches), lambda i: (0, 0)),
        ),
        compiler_params=pltpu.CompilerParams(vmem_limit_bytes=40 << 20),
    )(patch_ids, amplitudes[None], cotangent)


def local_kernel(scal, q, q_up, q_down, q_near, c, c_up, c_down, c_near, c_far, wall, coef, q_out, c_out):
    block, width = q.shape[1:]
    step, side = scal[0], scal[1]
    here, last = pl.program_id(0), pl.num_programs(0) - 1
    u, rd, ad = coef[:, 0:1], coef[:, 1:2], coef[:, 2:3]
    row = lax.broadcasted_iota(jnp.int32, (block, 1), 0)

    def around(x, up, down):
        above = jnp.where(row == 0, up, pltpu.roll(x, 1, 0))
        below = jnp.where(row == block - 1, down, pltpu.roll(x, block - 1, 0))
        return above, below

    def sides(x):
        return pltpu.roll(x, 1, 1) + pltpu.roll(x, width - 1, 1)

    x = q[0]
    first_row = pltpu.roll(x[:1], width // 2, 1)
    up = jnp.where(here == 0, first_row, q_up[0, SUB - 1 :])
    down = jnp.where(here == last, wall[...], q_down[0, :1])
    above, below = around(x, up, down)
    near = q_near[0]
    axial = near - (0.5 * side) * (near * (u + 0.5 * near)) - dissipation * x
    q_out[0] = x + step * (
        axial + rd * (above + below - 2.0 * x) + ad * (sides(x) - 2.0 * x)
    )

    y = c[0]
    weighted = rd * y
    before, after = coef_rows(coef)
    first_row = pltpu.roll(weighted[:1], width // 2, 1)
    up = jnp.where(here == 0, first_row, before * c_up[0, SUB - 1 :])
    down = jnp.where(here == last, 0.0, after * c_down[0, :1])
    above, below = around(weighted, up, down)
    slope = (0.5 * side) * (u + x)
    axial = c_near[0] * (1.0 + slope) + c_far[0] * (1.0 - slope) - dissipation * y
    c_out[0] = y + step * (
        axial + (above + below - 2.0 * weighted) + ad * (sides(y) - 2.0 * y)
    )


def coef_rows(coef):
    return coef[0:1, 3:4], coef[0:1, 4:5]


def local_parts(scal, q, q_near, c, c_near, c_far, wall, coef):
    rows, width = q.shape[1:]
    block = math.gcd(LOCAL_ROWS, rows)
    tiles, total = block // SUB, rows // SUB
    full = pl.BlockSpec((1, block, width), lambda i: (0, i, 0))
    up = pl.BlockSpec((1, SUB, width), lambda i: (0, jnp.maximum(i * tiles - 1, 0), 0))
    down = pl.BlockSpec((1, SUB, width), lambda i: (0, jnp.minimum((i + 1) * tiles, total - 1), 0))
    rd = coef[:, 1]
    before, after = jnp.roll(rd, 1), jnp.roll(rd, -block)
    coef = jnp.concatenate([coef, before[:, None], after[:, None]], axis=1)
    shape = jax.ShapeDtypeStruct(q.shape, q.dtype)
    return pl.pallas_call(
        local_kernel,
        grid=(rows // block,),
        out_shape=(shape, shape),
        in_specs=[pl.BlockSpec(memory_space=pltpu.SMEM)]
        + [full, up, down, full] * 2
        + [full]
        + [pl.BlockSpec((1, width), lambda i: (0, 0))]
        + [pl.BlockSpec((block, coef.shape[1]), lambda i: (i, 0))],
        out_specs=(full, full),
        compiler_params=pltpu.CompilerParams(vmem_limit_bytes=40 << 20),
        cost_estimate=pl.CostEstimate(
            flops=50 * rows * width, bytes_accessed=4 * rows * width * 7, transcendentals=0
        ),
    )(scal, q, q, q, q_near, c, c, c, c_near, c_far, wall, coef)


def state_far(base, far, weight, out):
    x = far[0]
    out[0] = base[0] + x * (weight[:, 0:1] + weight[:, 1:2] * x)


def add_rows(base, part, weight, start):
    rows, width = part.shape[1:]
    whole = rows <= ADD_ROWS and start % rows == 0
    block = rows if whole else math.gcd(ADD_ROWS, rows, start)
    first = start // block
    full = pl.BlockSpec((1, block, width), lambda i: (0, first + i, 0))
    piece = pl.BlockSpec((1, block, width), lambda i: (0, i, 0))
    column = pl.BlockSpec((block, weight.shape[1]), lambda i: (first + i, 0))
    return pl.pallas_call(
        state_far,
        grid=(rows // block,),
        out_shape=jax.ShapeDtypeStruct(base.shape, base.dtype),
        in_specs=[full, piece, column],
        out_specs=full,
        input_output_aliases={0: 0},
        compiler_params=pltpu.CompilerParams(vmem_limit_bytes=40 << 20),
        cost_estimate=pl.CostEstimate(
            flops=10 * rows * width, bytes_accessed=4 * rows * width * 3, transcendentals=0
        ),
    )(base, part, weight)


def put_rows(out, base, part, weight, start):
    rows, width = part.shape[1:]

    def kernel(base, far, weight, before, out, fresh, sem):
        x = far[0]
        of_row = weight[pl.ds(start, rows), :]
        fresh[...] = base[0] + x * (of_row[:, 0:1] + of_row[:, 1:2] * x)
        store = pltpu.make_async_copy(fresh, out.at[0, pl.ds(start, rows)], sem)
        store.start()
        store.wait()

    anywhere = pl.BlockSpec(memory_space=pl.ANY)
    return pl.pallas_call(
        kernel,
        out_shape=jax.ShapeDtypeStruct(out.shape, out.dtype),
        in_specs=[pl.BlockSpec(memory_space=pltpu.VMEM)] * 3 + [anywhere],
        out_specs=anywhere,
        scratch_shapes=[pltpu.VMEM((rows, width), jnp.float32), pltpu.SemaphoreType.DMA],
        input_output_aliases={3: 0},
        compiler_params=pltpu.CompilerParams(vmem_limit_bytes=40 << 20),
        cost_estimate=pl.CostEstimate(
            flops=10 * rows * width, bytes_accessed=4 * rows * width * 3, transcendentals=0
        ),
    )(base, part, weight, out)


def local(
    checkpoint,
    cotangent,
    amplitudes,
    patch_ids,
    substep,
    axial_speed,
    radial_diffusion,
    azimuth_diffusion,
):
    count = lax.axis_size("ax")
    rows = checkpoint.shape[1]
    patches = amplitudes.shape[0]
    near, far = on_pairs(count), off_pairs(count)
    cot_far_rows = lax.ppermute(cotangent, "ax", far)
    cot_near_rows = lax.ppermute(cotangent, "ax", near)
    state_near_rows = lax.ppermute(checkpoint, "ax", near)

    wall, binned = wall_and_bins(patch_ids, amplitudes, cotangent)
    if count & (count - 1) or count < 4:
        binned = lax.psum(binned, "ax")
    else:
        binned = cell_sum(binned, "ax")

    late, wall = lax.optimization_barrier((checkpoint, wall))
    edges = [rows * n // STATE_PARTS for n in STATE_CUTS]
    state_far_rows = [
        lax.ppermute(late[:, low:high], "ax", far) for low, high in zip(edges, edges[1:])
    ]

    step_size = section_size(substep)
    side = 1.0 - 2.0 * (lax.axis_index("ax") % 2).astype(jnp.float32)
    total_cells = checkpoint.shape[0] * count * checkpoint.shape[2]
    norm_factor = (patches / total_cells) ** 0.5
    gradient = (step_size * radial_diffusion[-1] * norm_factor) * binned[0]
    scal = jnp.stack([step_size, side])
    coef = jnp.stack([axial_speed, radial_diffusion, azimuth_diffusion], axis=1)
    half = 0.5 * side * step_size
    weight = jnp.stack(
        [step_size + half * axial_speed, jnp.broadcast_to(0.5 * half, axial_speed.shape)], axis=1
    )

    cot_far_rows, cot_near_rows, state_near_rows = lax.optimization_barrier(
        (cot_far_rows, cot_near_rows, state_near_rows)
    )
    advanced, adjoint = local_parts(
        scal, checkpoint, state_near_rows, cotangent, cot_near_rows, cot_far_rows, wall, coef
    )
    bases = [advanced[:, low:high] for low, high in zip(edges[1:], edges[2:])]
    advanced, *bases = lax.optimization_barrier((advanced, *bases))
    advanced = add_rows(advanced, state_far_rows[0], weight, 0)
    for low, base, part in zip(edges[1:], bases, state_far_rows[1:]):
        advanced = put_rows(advanced, base, part, weight, low)
    return (advanced, adjoint, gradient)


def solution(mesh):
    placed = (
        P(("case", "ax"), None, None),
        P(("case", "ax"), None, None),
        P("case"),
        P(("case", "ax"), None),
        P("case"),
        P(),
        P(),
        P(),
    )
    return jax.shard_map(
        local,
        mesh=mesh,
        in_specs=placed,
        out_specs=(P(("case", "ax"), None, None), P(("case", "ax"), None, None), P("case")),
        check_vma=False,
    )
```
